32 devices in a mesh: groups: 2 (over y), store: 4 (over z), tensor: 4 (over x, core).
Axes of the slice: x: 2, y: 2, z: 4, core: 2. Of those that a mesh axis runs over, the one named last changes fastest.
Arguments:
- states: bfloat16 [128, 6144], P(('groups', 'store')), parts along dimension 0, may hold values from -6 to 6
- weight_in: bfloat16 [6144, 24576], P('store', 'tensor'), may hold values from -0.078125 to 0.078125
- bias_in: float32 [24576], P('tensor'), may hold values from -3 to 3
- weight_out: bfloat16 [24576, 6144], P('tensor', 'store'), may hold values from -0.25 to 0.25
- bias_out: float32 [6144], P('tensor'), may hold values from -2 to 2
- block_lists: int32 [128, 4, 4], P(('groups', 'store'), 'tensor'), parts along dimension 0, may hold values from -1 to 47, as said below
- union_blocks: int32 [8, 16], P(('groups', 'tensor')), parts along dimension 0, may hold values from 0 to 47, as said below
Outputs:
- ffn_output: bfloat16 [128, 6144], P(('groups', 'store'), 'tensor'), parts along dimension 0
The draws below stay inside these ranges and needn't reach their ends.
There are 2 independent parts, one for each index of `groups`. The reference program is written for one: setup_inputs(seed, part) draws one part's arguments, and reference() takes and returns one part's arrays. A program takes and returns all parts, laid end to end along the dimension named above; an argument that names none is the same for every part. Nothing has to cross between parts.
Inputs may be any that keep to these rules, and one draw needn't show every extreme that they name: `block_lists`: for each row and slice the non-negative entries come first, are distinct, and all lie in union_blocks of that slice; every row has at least one; in every slice some row fills all 4 slots. `union_blocks`: each slice's 16 entries are distinct.
All inputs are finite; a program needn't handle non-finite values.
Results may differ from the reference program's by a relative error of at most 0.0048.
Values may be sent and summed in bfloat16 or wider, within the bound.
No kernel may reach another device: no remote copies, remote signals or barrier semaphores. Data moves between devices by JAX's collectives and lax.ppermute only.
A program may use at most 192 MiB of HBM per device.

```python
import jax
import jax.numpy as jnp

D = 6144
FF = 24576
BLOCK = 128
SLOTS = 4
UNION = 16
ROWS = 64
SLICES = 4
BLOCKS_SLICE = 48
N_TENSOR = 4


def union_from(key):
    base = jax.random.fold_in(key, 101)
    scores = jax.random.randint(base, (SLICES, BLOCKS_SLICE), 0, 2 ** 20) * BLOCKS_SLICE + jnp.arange(BLOCKS_SLICE, dtype=jnp.int32)[None, :]
    order = jnp.argsort(scores, axis=1)
    return order[:, :UNION].astype(jnp.int32)


def draw_union_blocks(key, part):
    return union_from(key)


def draw_block_lists(key, part):
    union_ids = union_from(key)
    key = jax.random.fold_in(key, 7)
    key_one, key_two, key_three, key_four = jax.random.split(key, 4)
    counts = jnp.minimum(jax.random.randint(key_one, (ROWS, SLICES), 1, SLOTS + 1), jax.random.randint(key_two, (ROWS, SLICES), 1, SLOTS + 1))
    full_row = jax.random.randint(key_three, (SLICES,), 0, ROWS)
    counts = jnp.where(jnp.arange(ROWS, dtype=jnp.int32)[:, None] == full_row[None, :], SLOTS, counts)
    scores = jax.random.randint(key_four, (ROWS, SLICES, UNION), 0, 2 ** 20) * UNION + jnp.arange(UNION, dtype=jnp.int32)[None, None, :]
    order = jnp.argsort(scores, axis=-1)[:, :, :SLOTS]
    spread_union = jnp.broadcast_to(union_ids[None, :, :], (ROWS, SLICES, UNION))
    chosen = jnp.take_along_axis(spread_union, order, axis=-1)
    chosen = jnp.where(jnp.arange(SLOTS, dtype=jnp.int32)[None, None, :] < counts[:, :, None], chosen, -1)
    return chosen.astype(jnp.int32)


def spiked(array, key, source, target, shards_of, factor):
    def block_of(dim):
        return (jnp.arange(array.shape[dim]) // (array.shape[dim] // shards_of)).reshape((-1,) + (1,) * (array.ndim - 1 - dim))

    first = jax.random.permutation(key, shards_of)[block_of(target)]
    other_side = (block_of(target) + shards_of // 2) % shards_of
    return jnp.where((block_of(source) == first) | (block_of(source) == other_side), factor * array, array)


def levels(key, dims, pieces, least, high):
    def one(axis_at, blocks):
        draws = jax.random.uniform(jax.random.fold_in(jax.random.fold_in(key, 6), axis_at), (blocks,), jnp.float32, least / len(pieces), high / len(pieces))
        return jnp.repeat(jnp.exp(draws), dims[axis_at] // blocks).reshape((-1,) + (1,) * (len(dims) - axis_at - 1))

    gain = one(*pieces[0])
    for cut in pieces[1:]:
        gain = gain * one(*cut)
    return gain


def bell_draw(key, dims, width, most, cuts=(), kind=jnp.bfloat16):
    values = jax.random.normal(key, dims, jnp.float32) * width
    if len(cuts) > 0:
        values = levels(key, dims, cuts, -0.22, 0.18) * values
    return jnp.clip(values, min=-most, max=most).astype(kind)


def bell_draw_with(rng, shape, width, reach, cuts, heavy, held_as=jnp.bfloat16):
    result = width * jax.random.normal(rng, shape, jnp.float32)
    if cuts:
        result = result * levels(rng, shape, cuts, -0.22, 0.18)
    return jnp.clip(spiked(result, jax.random.fold_in(rng, 3), *heavy), -reach, reach).astype(held_as)


def setup_inputs(seed: int = 0, part: int = 0) -> dict:
    arg_keys = jax.random.split(jax.random.key(seed), 8)
    part_splits = jax.random.split(jax.random.fold_in(arg_keys[7], part), 8)
    return {
        "states": bell_draw(part_splits[0], (ROWS, D), 1.0, 6.0, ((0, 4),)),
        "weight_in": bell_draw(arg_keys[1], (D, FF), D ** -0.5, 0.078125, ((0, 4), (1, 4))),
        "bias_in": bell_draw(arg_keys[2], (FF,), 0.5, 3.0, ((0, 4),), jnp.float32),
        "weight_out": bell_draw_with(arg_keys[3], (FF, D), (SLOTS * BLOCK * N_TENSOR // 2) ** -0.5, 0.25, ((0, 4), (1, 4)), (0, 1, 4, 2.0)),
        "bias_out": bell_draw(arg_keys[4], (D,), 0.3, 2.0, ((0, 4),), jnp.float32),
        "block_lists": draw_block_lists(jax.random.fold_in(jax.random.fold_in(arg_keys[7], part), 71), part),
        "union_blocks": draw_union_blocks(jax.random.fold_in(jax.random.fold_in(arg_keys[7], part), 71), part),
    }


def reference(states, weight_in, bias_in, weight_out, bias_out, block_lists, union_blocks):
    nblocks = FF // BLOCK
    offsets = (jnp.arange(SLICES, dtype=jnp.int32) * BLOCKS_SLICE)[None, :, None]
    in_union = jnp.any(union_blocks[:, :, None] == jnp.arange(BLOCKS_SLICE, dtype=jnp.int32)[None, None, :], axis=1).reshape(nblocks)
    global_ids = jnp.where(block_lists >= 0, block_lists + offsets, -1).reshape(ROWS, SLICES * SLOTS)
    listed = jnp.any(global_ids[:, :, None] == jnp.arange(nblocks, dtype=jnp.int32)[None, None, :], axis=1)
    active = jnp.logical_and(listed, in_union[None, :]).astype(jnp.float32)
    active_mask = jnp.repeat(active, BLOCK, axis=1)
    pre_act = jnp.dot(states, weight_in, preferred_element_type=jnp.float32)
    hidden = (jnp.maximum(pre_act + bias_in.astype(jnp.float32)[None, :], 0.0) * active_mask).astype(jnp.bfloat16)
    output = jnp.dot(hidden, weight_out, preferred_element_type=jnp.float32) + bias_out.astype(jnp.float32)[None, :]
    return output.astype(jnp.bfloat16)
```

```python
import functools

import jax
import jax.numpy as jnp
from jax import lax
from jax.experimental import pallas as pl
from jax.experimental.pallas import tpu as pltpu
from jax.sharding import PartitionSpec as P

BLOCK = 128
BF16 = jnp.bfloat16
F32 = jnp.float32
VMEM = pltpu.VMEM
SMEM = pltpu.SMEM


def whole(space):
    return pl.BlockSpec(memory_space=space)


def split_kernel(count, width, me_ref, states_ref, ids_ref, *out_refs):
    me = me_ref[0]
    slots = ids_ref.shape[1]
    for k in range(count):
        start = pl.multiple_of((me ^ k) * width, BLOCK)
        out_refs[k][:, :width] = states_ref[:, pl.ds(start, width)]
        out_refs[k][:, width:] = jnp.zeros((states_ref.shape[0], BLOCK), BF16)
        out_refs[k][:, width : width + slots] = ids_ref[...].astype(F32).astype(BF16)


def gather_kernel(union_ref, win_ref, wout_ref, win_out, wout_out, sems):
    union = union_ref.shape[0]
    for u in range(union):
        start = pl.multiple_of(union_ref[u] * BLOCK, BLOCK)
        pltpu.make_async_copy(
            win_ref.at[:, pl.ds(start, BLOCK)], win_out.at[:, pl.ds(u * BLOCK, BLOCK)], sems.at[0, u]
        ).start()
    for u in range(union):
        start = pl.multiple_of(union_ref[u] * BLOCK, BLOCK)
        pltpu.make_async_copy(
            wout_ref.at[pl.ds(start, BLOCK), :], wout_out.at[pl.ds(u * BLOCK, BLOCK), :], sems.at[1, u]
        ).start()
    for u in range(union):
        start = pl.multiple_of(union_ref[u] * BLOCK, BLOCK)
        pltpu.make_async_copy(
            win_ref.at[:, pl.ds(start, BLOCK)], win_out.at[:, pl.ds(u * BLOCK, BLOCK)], sems.at[0, u]
        ).wait()
        pltpu.make_async_copy(
            wout_ref.at[pl.ds(start, BLOCK), :], wout_out.at[pl.ds(u * BLOCK, BLOCK), :], sems.at[1, u]
        ).wait()


def first_kernel(count, slots, union_ref, *refs):
    chunk_refs = refs[:count]
    win_ref, pre_ref, ids_ref, dense = refs[count:]
    width, total = win_ref.shape
    rows = chunk_refs[0].shape[0]
    union = union_ref.shape[0]
    states = jnp.concatenate([c[:, :width] for c in chunk_refs], axis=0)
    ids = jnp.concatenate([c[:, width:] for c in chunk_refs], axis=0).astype(F32)
    ids_ref[...] = ids
    step = 2 * BLOCK
    for n in range(0, total, step):
        dense[:, n : n + step] = jnp.dot(states, win_ref[:, n : n + step], preferred_element_type=F32)
    for j in range(count):
        part = slice(j * rows, (j + 1) * rows)
        for k in range(slots):
            mine = jnp.broadcast_to(ids[part, k : k + 1], (rows, BLOCK))
            picked = jnp.zeros((rows, BLOCK), F32)
            for u in range(union):
                block = union_ref[u].astype(F32)
                picked = jnp.where(mine == block, dense[part, u * BLOCK : (u + 1) * BLOCK], picked)
            pre_ref[part, k * BLOCK : (k + 1) * BLOCK] = picked.astype(pre_ref.dtype)


def second_kernel(count, slots, me_ref, union_ref, ids_ref, bias_ref, *refs):
    part_refs = refs[:count]
    wout_ref = refs[count]
    out_refs = refs[count + 1 : 2 * count + 1]
    spread, terms = refs[2 * count + 1 :]
    store, tensor = me_ref[0], me_ref[1]
    rows = ids_ref.shape[0] // count
    union = union_ref.shape[0]
    ids = ids_ref[...]
    for j in range(count):
        part = slice(j * rows, (j + 1) * rows)
        mines = [jnp.broadcast_to(ids[part, k : k + 1], (rows, BLOCK)) for k in range(slots)]
        pres = []
        for k in range(slots):
            cols = slice(k * BLOCK, (k + 1) * BLOCK)
            pres.append(sum(p[part, cols].astype(F32) for p in part_refs))
        for u in range(union):
            block = union_ref[u].astype(F32)
            value = jnp.zeros((rows, BLOCK), F32)
            bias = bias_ref[pl.ds(union_ref[u], 1), :]
            for k in range(slots):
                value = jnp.where(mines[k] == block, jnp.maximum(pres[k] + bias, 0.0), value)
            spread[part, u * BLOCK : (u + 1) * BLOCK] = value.astype(BF16)
    step = 2 * BLOCK
    width = wout_ref.shape[1]
    hidden = spread[...]
    for n in range(0, width, step):
        product = jnp.dot(hidden, wout_ref[:, n : n + step], preferred_element_type=F32)
        terms[:, :, n : n + step] = product.reshape(count, rows, step)
    for k in range(count):
        out_refs[k][...] = terms[store ^ tensor ^ k].astype(out_refs[k].dtype)


def fast(states, weight_in, bias_in, weight_out, bias_out, block_lists, union_blocks):
    count = lax.axis_size("store")
    width = weight_in.shape[0]
    rows = states.shape[0]
    slots = block_lists.shape[2]
    union_ids = union_blocks[0]
    union = union_ids.shape[0]
    me = jnp.stack([lax.axis_index("store"), lax.axis_index("tensor")]).astype(jnp.int32)
    total = union * BLOCK

    chunks = pl.pallas_call(
        functools.partial(split_kernel, count, width),
        out_shape=[jax.ShapeDtypeStruct((rows, width + BLOCK), BF16)] * count,
        in_specs=[whole(SMEM), whole(VMEM), whole(VMEM)],
        out_specs=[whole(VMEM)] * count,
        name="split_states",
    )(me, states, block_lists[:, 0, :])

    def over_store(k):
        return [(i, i ^ k) for i in range(count)]

    got = [chunks[0]] + [lax.ppermute(chunks[k], "store", over_store(k)) for k in range(1, count)]

    win, wout = pl.pallas_call(
        gather_kernel,
        out_shape=[VMEM((width, total), BF16), VMEM((total, width), BF16)],
        in_specs=[whole(SMEM), whole(pl.ANY), whole(pl.ANY)],
        out_specs=[whole(VMEM), whole(VMEM)],
        scratch_shapes=[pltpu.SemaphoreType.DMA((2, union))],
        compiler_params=pltpu.CompilerParams(vmem_limit_bytes=40 * 2**20),
        cost_estimate=pl.CostEstimate(flops=0, bytes_accessed=4 * width * total, transcendentals=0),
        name="gather_weights",
    )(union_ids, weight_in, weight_out)

    pre, ids = pl.pallas_call(
        functools.partial(first_kernel, count, slots),
        out_shape=[
            jax.ShapeDtypeStruct((count * rows, slots * BLOCK), BF16),
            jax.ShapeDtypeStruct((count * rows, BLOCK), F32),
        ],
        in_specs=[whole(SMEM)] + [whole(VMEM)] * (count + 1),
        out_specs=[whole(VMEM)] * 2,
        scratch_shapes=[VMEM((count * rows, total), F32)],
        compiler_params=pltpu.CompilerParams(vmem_limit_bytes=40 * 2**20),
        name="first_dot",
    )(union_ids, *got, win)

    def reorder(a, k):
        blocks = a.reshape(count, rows, a.shape[1])
        return jnp.concatenate([blocks[j ^ k] for j in range(count)], axis=0)

    parts = [pre] + [reorder(lax.ppermute(pre, "store", over_store(k)), k) for k in range(1, count)]

    terms = pl.pallas_call(
        functools.partial(second_kernel, count, slots),
        out_shape=[jax.ShapeDtypeStruct((rows, width), F32)] * count,
        in_specs=[whole(SMEM), whole(SMEM)] + [whole(VMEM)] * (count + 3),
        out_specs=[whole(VMEM)] * count,
        scratch_shapes=[VMEM((count * rows, total), BF16), VMEM((count, rows, width), F32)],
        compiler_params=pltpu.CompilerParams(vmem_limit_bytes=40 * 2**20),
        name="second_dot",
    )(me, union_ids, ids, bias_in.reshape(-1, BLOCK), *parts, wout)

    def home(k):
        return [(s * count + t, (t ^ k) * count + s) for s in range(count) for t in range(count)]

    summed = sum(lax.ppermute(terms[k], ("store", "tensor"), home(k)) for k in range(count))
    return (summed + bias_out[None, :]).astype(BF16)


def general(states, weight_in, bias_in, weight_out, bias_out, block_lists, union_blocks):
    slice_width = weight_in.shape[0]
    union_ids = union_blocks[0]
    union_count = union_ids.shape[0]
    block_count = weight_in.shape[1] // BLOCK
    slot_count = block_lists.shape[2]
    own_rows = states.shape[0]
    sliced_states = lax.all_to_all(states, "store", split_axis=1, concat_axis=0, tiled=True)
    all_ids = lax.all_gather(block_lists, "store", axis=0, tiled=True)[:, 0, :]
    union_range = jnp.arange(union_count, dtype=jnp.int32)
    all_match = all_ids[:, :, None] == union_ids[None, None, :]
    all_keep = jnp.any(all_match, axis=-1)
    slot_pos = jnp.sum(jnp.where(all_match, union_range[None, None, :], 0), axis=-1)
    weight_in_union = jnp.take(
        weight_in.reshape(slice_width, block_count, BLOCK), union_ids, axis=1
    ).reshape(slice_width, union_count * BLOCK)
    weight_out_union = jnp.take(
        weight_out.reshape(block_count, BLOCK, slice_width), union_ids, axis=0
    ).reshape(union_count * BLOCK, slice_width)
    bias_blocks = bias_in.reshape(block_count, BLOCK)
    dense_pre = jnp.dot(sliced_states, weight_in_union, preferred_element_type=F32).reshape(
        own_rows * lax.axis_size("store"), union_count, BLOCK
    )
    picked = jnp.take_along_axis(dense_pre, slot_pos[:, :, None], axis=1)
    pre_act = lax.psum_scatter(
        (picked * all_keep[:, :, None].astype(F32)).reshape(
            own_rows * lax.axis_size("store"), slot_count * BLOCK
        ),
        "store",
        scatter_dimension=0,
        tiled=True,
    )
    own_ids = block_lists[:, 0, :]
    own_keep = jnp.any(own_ids[:, :, None] == union_ids[None, None, :], axis=-1)
    bias_rows = jnp.take(bias_blocks, jnp.maximum(own_ids, 0), axis=0).reshape(
        own_ids.shape[0], slot_count * BLOCK
    )
    active_mask = jnp.repeat(own_keep.astype(F32), BLOCK, axis=1)
    hidden = (jnp.maximum(pre_act + bias_rows, 0.0) * active_mask).astype(BF16)
    project_hidden = lax.all_gather(hidden, "store", axis=0, tiled=True)
    one_hot = jnp.logical_and(
        slot_pos[:, :, None] == union_range[None, None, :], all_keep[:, :, None]
    ).astype(BF16)
    spread = jnp.einsum(
        "rku,rkn->run",
        one_hot,
        project_hidden.reshape(-1, slot_count, BLOCK),
        preferred_element_type=F32,
    ).astype(BF16)
    partial_value = jnp.dot(
        spread.reshape(-1, union_count * BLOCK), weight_out_union, preferred_element_type=F32
    )
    row_terms = lax.all_to_all(partial_value, "store", split_axis=0, concat_axis=1, tiled=True)
    summed = lax.psum_scatter(row_terms, "tensor", scatter_dimension=1, tiled=True)
    return (summed + bias_out[None, :]).astype(BF16)


def solution(mesh):
    count = mesh.shape["store"]
    square = count == mesh.shape["tensor"] and count & (count - 1) == 0
    return jax.shard_map(
        fast if square else general,
        mesh=mesh,
        in_specs=(
            P(("groups", "store"), None),
            P("store", "tensor"),
            P("tensor"),
            P("tensor", "store"),
            P("tensor"),
            P(("groups", "store"), "tensor", None),
            P(("groups", "tensor"), None),
        ),
        out_specs=P(("groups", "store"), "tensor"),
        check_vma=False,
    )
```

```python
import functools

import jax
import jax.numpy as jnp
from jax import lax
from jax.experimental import pallas as pl
from jax.experimental.pallas import tpu as pltpu
from jax.sharding import PartitionSpec as P

BLOCK = 128
BF16 = jnp.bfloat16
F32 = jnp.float32
VMEM = pltpu.VMEM
SMEM = pltpu.SMEM


def whole(space):
    return pl.BlockSpec(memory_space=space)


def split_kernel(count, width, states_ref, ids_ref, *refs):
    out_refs, sems = refs[:count], refs[count]
    me = lax.axis_index("store")
    copies = []
    for k in range(count):
        start = pl.multiple_of((me ^ k) * width, BLOCK)
        copies.append(
            pltpu.make_async_copy(
                states_ref.at[:, pl.ds(start, width)], out_refs[k].at[:, :width], sems.at[k]
            )
        )
    for k in list(range(1, count)) + [0]:
        copies[k].start()
    slots, rows = ids_ref.shape
    ids = ids_ref[...].astype(F32)
    padded = jnp.concatenate([ids, jnp.full((BLOCK - slots, rows), -1.0, F32)], axis=0)
    tail = padded.T.astype(BF16)
    for k in range(count):
        out_refs[k][:, width:] = tail
    for k in range(count):
        copies[k].wait()


def gather_kernel(by_column, union_ref, weight_ref, out_ref, sems):
    copies = []
    for u in range(union_ref.shape[0]):
        block = pl.ds(pl.multiple_of(union_ref[u] * BLOCK, BLOCK), BLOCK)
        place = pl.ds(u * BLOCK, BLOCK)
        if by_column:
            source, target = weight_ref.at[:, block], out_ref.at[:, place]
        else:
            source, target = weight_ref.at[block, :], out_ref.at[place, :]
        copies.append(pltpu.make_async_copy(source, target, sems.at[u]))
        copies[-1].start()
    for copy in copies:
        copy.wait()


def gather(by_column, union_ids, weight, name):
    union = union_ids.shape[0]
    shape = (weight.shape[0], union * BLOCK) if by_column else (union * BLOCK, weight.shape[1])
    return pl.pallas_call(
        functools.partial(gather_kernel, by_column),
        out_shape=VMEM(shape, BF16),
        in_specs=[whole(SMEM), whole(pltpu.HBM)],
        out_specs=whole(VMEM),
        scratch_shapes=[pltpu.SemaphoreType.DMA((union,))],
        compiler_params=pltpu.CompilerParams(vmem_limit_bytes=40 * 2**20),
        cost_estimate=pl.CostEstimate(flops=0, bytes_accessed=4 * shape[0] * shape[1], transcendentals=0),
        name=name,
    )(union_ids, weight)


def first_kernel(count, slots, union_ref, *refs):
    chunk_refs = refs[:count]
    win_ref, pre_ref, ids_ref, dense = refs[count:]
    width, total = win_ref.shape
    rows = chunk_refs[0].shape[0]
    union = union_ref.shape[0]
    states = jnp.concatenate([c[:, :width] for c in chunk_refs], axis=0)
    ids = jnp.concatenate([c[:, width:] for c in chunk_refs], axis=0).astype(F32)
    ids_ref[...] = ids
    step = 2 * BLOCK
    for n in range(0, total, step):
        dense[:, n : n + step] = jnp.dot(states, win_ref[:, n : n + step], preferred_element_type=F32)
    for j in range(count):
        part = slice(j * rows, (j + 1) * rows)
        for k in range(slots):
            mine = jnp.broadcast_to(ids[part, k : k + 1], (rows, BLOCK))
            picked = jnp.zeros((rows, BLOCK), F32)
            for u in range(union):
                block = union_ref[u].astype(F32)
                picked = jnp.where(mine == block, dense[part, u * BLOCK : (u + 1) * BLOCK], picked)
            pre_ref[part, k * BLOCK : (k + 1) * BLOCK] = picked.astype(pre_ref.dtype)


def second_kernel(count, slots, union_ref, ids_ref, bias_ref, *refs):
    part_refs = refs[:count]
    wout_ref = refs[count]
    out_refs = refs[count + 1 : 2 * count + 1]
    spread, terms = refs[2 * count + 1 :]
    store, tensor = lax.axis_index("store"), lax.axis_index("tensor")
    rows = ids_ref.shape[0] // count
    union = union_ref.shape[0]
    ids = ids_ref[...]
    for j in range(count):
        part = slice(j * rows, (j + 1) * rows)
        mines = [jnp.broadcast_to(ids[part, k : k + 1], (rows, BLOCK)) for k in range(slots)]
        pres = []
        for k in range(slots):
            cols = slice(k * BLOCK, (k + 1) * BLOCK)
            pres.append(sum(p[part, cols].astype(F32) for p in part_refs))
        for u in range(union):
            block = union_ref[u].astype(F32)
            value = jnp.zeros((rows, BLOCK), F32)
            bias = bias_ref[pl.ds(union_ref[u], 1), :]
            for k in range(slots):
                value = jnp.where(mines[k] == block, jnp.maximum(pres[k] + bias, 0.0), value)
            spread[part, u * BLOCK : (u + 1) * BLOCK] = value.astype(BF16)
    step = 2 * BLOCK
    width = wout_ref.shape[1]
    hidden = spread[...]
    for n in range(0, width, step):
        product = jnp.dot(hidden, wout_ref[:, n : n + step], preferred_element_type=F32)
        terms[:, :, n : n + step] = product.reshape(count, rows, step)
    for k in range(count):
        out_refs[k][...] = terms[store ^ tensor ^ k].astype(out_refs[k].dtype)


def fast(states, weight_in, bias_in, weight_out, bias_out, block_lists, union_blocks):
    count = lax.axis_size("store")
    width = weight_in.shape[0]
    rows = states.shape[0]
    slots = block_lists.shape[2]
    union_ids = union_blocks[0]
    union = union_ids.shape[0]
    total = union * BLOCK

    chunks = pl.pallas_call(
        functools.partial(split_kernel, count, width),
        out_shape=[jax.ShapeDtypeStruct((rows, width + BLOCK), BF16)] * count,
        in_specs=[whole(pltpu.HBM), whole(VMEM)],
        out_specs=[whole(VMEM)] * count,
        scratch_shapes=[pltpu.SemaphoreType.DMA((count,))],
        name="split_states",
    )(states, jnp.transpose(block_lists, (1, 2, 0))[0])

    def over_store(k):
        return [(i, i ^ k) for i in range(count)]

    got = [chunks[0]] + [lax.ppermute(chunks[k], "store", over_store(k)) for k in range(1, count)]

    win = gather(True, union_ids, weight_in, "gather_in")

    pre, ids = pl.pallas_call(
        functools.partial(first_kernel, count, slots),
        out_shape=[
            jax.ShapeDtypeStruct((count * rows, slots * BLOCK), BF16),
            jax.ShapeDtypeStruct((count * rows, BLOCK), F32),
        ],
        in_specs=[whole(SMEM)] + [whole(VMEM)] * (count + 1),
        out_specs=[whole(VMEM)] * 2,
        scratch_shapes=[VMEM((count * rows, total), F32)],
        compiler_params=pltpu.CompilerParams(vmem_limit_bytes=40 * 2**20),
        name="first_dot",
    )(union_ids, *got, win)

    def reorder(a, k):
        blocks = a.reshape(count, rows, a.shape[1])
        return jnp.concatenate([blocks[j ^ k] for j in range(count)], axis=0)

    parts = [pre] + [reorder(lax.ppermute(pre, "store", over_store(k)), k) for k in range(1, count)]

    wout = gather(False, union_ids, weight_out, "gather_out")

    terms = pl.pallas_call(
        functools.partial(second_kernel, count, slots),
        out_shape=[jax.ShapeDtypeStruct((rows, width), BF16)] * count,
        in_specs=[whole(SMEM)] + [whole(VMEM)] * (count + 3),
        out_specs=[whole(VMEM)] * count,
        scratch_shapes=[VMEM((count * rows, total), BF16), VMEM((count, rows, width), F32)],
        compiler_params=pltpu.CompilerParams(vmem_limit_bytes=40 * 2**20),
        name="second_dot",
    )(union_ids, ids, bias_in.reshape(-1, BLOCK), *parts, wout)

    def home(k):
        return [(s * count + t, (t ^ k) * count + s) for s in range(count) for t in range(count)]

    summed = sum(lax.ppermute(terms[k], ("store", "tensor"), home(k)).astype(F32) for k in range(count))
    return (summed + bias_out[None, :]).astype(BF16)


def general(states, weight_in, bias_in, weight_out, bias_out, block_lists, union_blocks):
    slice_width = weight_in.shape[0]
    union_ids = union_blocks[0]
    union_count = union_ids.shape[0]
    block_count = weight_in.shape[1] // BLOCK
    slot_count = block_lists.shape[2]
    own_rows = states.shape[0]
    sliced_states = lax.all_to_all(states, "store", split_axis=1, concat_axis=0, tiled=True)
    all_ids = lax.all_gather(block_lists, "store", axis=0, tiled=True)[:, 0, :]
    union_range = jnp.arange(union_count, dtype=jnp.int32)
    all_match = all_ids[:, :, None] == union_ids[None, None, :]
    all_keep = jnp.any(all_match, axis=-1)
    slot_pos = jnp.sum(jnp.where(all_match, union_range[None, None, :], 0), axis=-1)
    weight_in_union = jnp.take(
        weight_in.reshape(slice_width, block_count, BLOCK), union_ids, axis=1
    ).reshape(slice_width, union_count * BLOCK)
    weight_out_union = jnp.take(
        weight_out.reshape(block_count, BLOCK, slice_width), union_ids, axis=0
    ).reshape(union_count * BLOCK, slice_width)
    bias_blocks = bias_in.reshape(block_count, BLOCK)
    dense_pre = jnp.dot(sliced_states, weight_in_union, preferred_element_type=F32).reshape(
        own_rows * lax.axis_size("store"), union_count, BLOCK
    )
    picked = jnp.take_along_axis(dense_pre, slot_pos[:, :, None], axis=1)
    pre_act = lax.psum_scatter(
        (picked * all_keep[:, :, None].astype(F32)).reshape(
            own_rows * lax.axis_size("store"), slot_count * BLOCK
        ),
        "store",
        scatter_dimension=0,
        tiled=True,
    )
    own_ids = block_lists[:, 0, :]
    own_keep = jnp.any(own_ids[:, :, None] == union_ids[None, None, :], axis=-1)
    bias_rows = jnp.take(bias_blocks, jnp.maximum(own_ids, 0), axis=0).reshape(
        own_ids.shape[0], slot_count * BLOCK
    )
    active_mask = jnp.repeat(own_keep.astype(F32), BLOCK, axis=1)
    hidden = (jnp.maximum(pre_act + bias_rows, 0.0) * active_mask).astype(BF16)
    project_hidden = lax.all_gather(hidden, "store", axis=0, tiled=True)
    one_hot = jnp.logical_and(
        slot_pos[:, :, None] == union_range[None, None, :], all_keep[:, :, None]
    ).astype(BF16)
    spread = jnp.einsum(
        "rku,rkn->run",
        one_hot,
        project_hidden.reshape(-1, slot_count, BLOCK),
        preferred_element_type=F32,
    ).astype(BF16)
    partial_value = jnp.dot(
        spread.reshape(-1, union_count * BLOCK), weight_out_union, preferred_element_type=F32
    )
    row_terms = lax.all_to_all(partial_value, "store", split_axis=0, concat_axis=1, tiled=True)
    summed = lax.psum_scatter(row_terms, "tensor", scatter_dimension=1, tiled=True)
    return (summed + bias_out[None, :]).astype(BF16)


def solution(mesh):
    count = mesh.shape["store"]
    square = count == mesh.shape["tensor"] and count & (count - 1) == 0
    return jax.shard_map(
        fast if square else general,
        mesh=mesh,
        in_specs=(
            P(("groups", "store"), None),
            P("store", "tensor"),
            P("tensor"),
            P("tensor", "store"),
            P("tensor"),
            P(("groups", "store"), "tensor", None),
            P(("groups", "tensor"), None),
        ),
        out_specs=P(("groups", "store"), "tensor"),
        check_vma=False,
    )
```

```python
import functools

import jax
import jax.numpy as jnp
from jax import lax
from jax.experimental import pallas as pl
from jax.experimental.pallas import tpu as pltpu
from jax.sharding import PartitionSpec as P

BLOCK = 128
BF16 = jnp.bfloat16
F32 = jnp.float32
VMEM = pltpu.VMEM
SMEM = pltpu.SMEM


def whole(space):
    return pl.BlockSpec(memory_space=space)


def split_kernel(count, width, states_ref, ids_ref, union_ref, *refs):
    out_refs, union_out, ids, sems = refs[:count], refs[count], refs[count + 1], refs[count + 2]
    me = lax.axis_index("store")
    ids_copy = pltpu.make_async_copy(ids_ref, ids, sems.at[count])
    ids_copy.start()
    copies = []
    for k in list(range(1, count)) + [0]:
        start = pl.multiple_of((me ^ k) * width, BLOCK)
        copies.append(
            pltpu.make_async_copy(
                states_ref.at[:, pl.ds(start, width)], out_refs[k].at[:, :width], sems.at[k]
            )
        )
        copies[-1].start()
    copies.append(pltpu.make_async_copy(union_ref, union_out, sems.at[count + 1]))
    copies[-1].start()
    slots, rows = ids_ref.shape
    ids_copy.wait()
    padded = jnp.concatenate(
        [ids[...].astype(F32), jnp.full((BLOCK - slots, rows), -1.0, F32)], axis=0
    )
    tail = padded.T.astype(BF16)
    for k in range(count):
        out_refs[k][:, width:] = tail
    for copy in copies:
        copy.wait()


def gather_kernel(by_column, union_ref, weight_ref, out_ref, sems):
    copies = []
    for u in range(union_ref.shape[0]):
        block = pl.ds(pl.multiple_of(union_ref[u] * BLOCK, BLOCK), BLOCK)
        place = pl.ds(u * BLOCK, BLOCK)
        if by_column:
            source, target = weight_ref.at[:, block], out_ref.at[:, place]
        else:
            source, target = weight_ref.at[block, :], out_ref.at[place, :]
        copies.append(pltpu.make_async_copy(source, target, sems.at[u]))
        copies[-1].start()
    for copy in copies:
        copy.wait()


def gather(by_column, union_ids, weight, name):
    union = union_ids.shape[0]
    shape = (weight.shape[0], union * BLOCK) if by_column else (union * BLOCK, weight.shape[1])
    return pl.pallas_call(
        functools.partial(gather_kernel, by_column),
        out_shape=VMEM(shape, BF16),
        in_specs=[whole(SMEM), whole(pltpu.HBM)],
        out_specs=whole(VMEM),
        scratch_shapes=[pltpu.SemaphoreType.DMA((union,))],
        compiler_params=pltpu.CompilerParams(vmem_limit_bytes=40 * 2**20),
        cost_estimate=pl.CostEstimate(flops=0, bytes_accessed=4 * shape[0] * shape[1], transcendentals=0),
        name=name,
    )(union_ids, weight)


def first_kernel(count, slots, union_ref, *refs):
    chunk_refs = refs[:count]
    win_ref, pre_ref, ids_ref, dense = refs[count:]
    width, total = win_ref.shape
    rows = chunk_refs[0].shape[0]
    union = union_ref.shape[0]
    states = jnp.concatenate([c[:, :width] for c in chunk_refs], axis=0)
    ids = jnp.concatenate([c[:, width:] for c in chunk_refs], axis=0).astype(F32)
    ids_ref[...] = ids
    step = 2 * BLOCK
    for n in range(0, total, step):
        dense[:, n : n + step] = jnp.dot(states, win_ref[:, n : n + step], preferred_element_type=F32)
    for j in range(count):
        part = slice(j * rows, (j + 1) * rows)
        for k in range(slots):
            mine = jnp.broadcast_to(ids[part, k : k + 1], (rows, BLOCK))
            picked = jnp.zeros((rows, BLOCK), F32)
            for u in range(union):
                block = union_ref[u].astype(F32)
                picked = jnp.where(mine == block, dense[part, u * BLOCK : (u + 1) * BLOCK], picked)
            pre_ref[part, k * BLOCK : (k + 1) * BLOCK] = picked.astype(pre_ref.dtype)


def second_kernel(count, slots, union_ref, ids_ref, bias_ref, *refs):
    part_refs = refs[:count]
    wout_ref = refs[count]
    out_refs = refs[count + 1 : 2 * count + 1]
    spread, terms = refs[2 * count + 1 :]
    store, tensor = lax.axis_index("store"), lax.axis_index("tensor")
    rows = ids_ref.shape[0] // count
    union = union_ref.shape[0]
    ids = ids_ref[...]
    for j in range(count):
        part = slice(j * rows, (j + 1) * rows)
        mines = [jnp.broadcast_to(ids[part, k : k + 1], (rows, BLOCK)) for k in range(slots)]
        pres = []
        for k in range(slots):
            cols = slice(k * BLOCK, (k + 1) * BLOCK)
            pres.append(
                sum(
                    p[(j ^ i) * rows : ((j ^ i) + 1) * rows, cols].astype(F32)
                    for i, p in enumerate(part_refs)
                )
            )
        for u in range(union):
            block = union_ref[u].astype(F32)
            value = jnp.zeros((rows, BLOCK), F32)
            bias = bias_ref[pl.ds(union_ref[u], 1), :]
            for k in range(slots):
                value = jnp.where(mines[k] == block, jnp.maximum(pres[k] + bias, 0.0), value)
            spread[part, u * BLOCK : (u + 1) * BLOCK] = value.astype(BF16)
    step = 2 * BLOCK
    width = wout_ref.shape[1]
    hidden = spread[...]
    for n in range(0, width, step):
        product = jnp.dot(hidden, wout_ref[:, n : n + step], preferred_element_type=F32)
        terms[:, :, n : n + step] = product.reshape(count, rows, step)
    for k in range(count):
        out_refs[k][...] = terms[store ^ tensor ^ k].astype(out_refs[k].dtype)


def fast(states, weight_in, bias_in, weight_out, bias_out, block_lists, union_blocks):
    count = lax.axis_size("store")
    width = weight_in.shape[0]
    rows = states.shape[0]
    slots = block_lists.shape[2]
    union = union_blocks.shape[1]
    total = union * BLOCK

    *chunks, union_ids = pl.pallas_call(
        functools.partial(split_kernel, count, width),
        out_shape=[jax.ShapeDtypeStruct((rows, width + BLOCK), BF16)] * count
        + [jax.ShapeDtypeStruct(union_blocks.shape, jnp.int32)],
        in_specs=[whole(pltpu.HBM)] * 3,
        out_specs=[whole(VMEM)] * (count + 1),
        scratch_shapes=[VMEM((slots, rows), jnp.int32), pltpu.SemaphoreType.DMA((count + 2,))],
        name="split_states",
    )(states, jnp.transpose(block_lists, (1, 2, 0))[0], union_blocks)
    union_ids = union_ids[0]

    def over_store(k):
        return [(i, i ^ k) for i in range(count)]

    got = [chunks[0]] + [lax.ppermute(chunks[k], "store", over_store(k)) for k in range(1, count)]

    win = gather(True, union_ids, weight_in, "gather_in")

    pre, ids = pl.pallas_call(
        functools.partial(first_kernel, count, slots),
        out_shape=[
            jax.ShapeDtypeStruct((count * rows, slots * BLOCK), BF16),
            jax.ShapeDtypeStruct((count * rows, BLOCK), F32),
        ],
        in_specs=[whole(SMEM)] + [whole(VMEM)] * (count + 1),
        out_specs=[whole(VMEM)] * 2,
        scratch_shapes=[VMEM((count * rows, total), F32)],
        compiler_params=pltpu.CompilerParams(vmem_limit_bytes=40 * 2**20),
        name="first_dot",
    )(union_ids, *got, win)

    parts = [pre] + [lax.ppermute(pre, "store", over_store(k)) for k in range(1, count)]

    wout = gather(False, union_ids, weight_out, "gather_out")

    terms = pl.pallas_call(
        functools.partial(second_kernel, count, slots),
        out_shape=[jax.ShapeDtypeStruct((rows, width), BF16)] * count,
        in_specs=[whole(SMEM)] + [whole(VMEM)] * (count + 3),
        out_specs=[whole(VMEM)] * count,
        scratch_shapes=[VMEM((count * rows, total), BF16), VMEM((count, rows, width), F32)],
        compiler_params=pltpu.CompilerParams(vmem_limit_bytes=40 * 2**20),
        name="second_dot",
    )(union_ids, ids, bias_in.reshape(-1, BLOCK), *parts, wout)

    def home(k):
        return [(s * count + t, (t ^ k) * count + s) for s in range(count) for t in range(count)]

    summed = sum(lax.ppermute(terms[k], ("store", "tensor"), home(k)).astype(F32) for k in range(count))
    return (summed + bias_out[None, :]).astype(BF16)


def general(states, weight_in, bias_in, weight_out, bias_out, block_lists, union_blocks):
    slice_width = weight_in.shape[0]
    union_ids = union_blocks[0]
    union_count = union_ids.shape[0]
    block_count = weight_in.shape[1] // BLOCK
    slot_count = block_lists.shape[2]
    own_rows = states.shape[0]
    sliced_states = lax.all_to_all(states, "store", split_axis=1, concat_axis=0, tiled=True)
    all_ids = lax.all_gather(block_lists, "store", axis=0, tiled=True)[:, 0, :]
    union_range = jnp.arange(union_count, dtype=jnp.int32)
    all_match = all_ids[:, :, None] == union_ids[None, None, :]
    all_keep = jnp.any(all_match, axis=-1)
    slot_pos = jnp.sum(jnp.where(all_match, union_range[None, None, :], 0), axis=-1)
    weight_in_union = jnp.take(
        weight_in.reshape(slice_width, block_count, BLOCK), union_ids, axis=1
    ).reshape(slice_width, union_count * BLOCK)
    weight_out_union = jnp.take(
        weight_out.reshape(block_count, BLOCK, slice_width), union_ids, axis=0
    ).reshape(union_count * BLOCK, slice_width)
    bias_blocks = bias_in.reshape(block_count, BLOCK)
    dense_pre = jnp.dot(sliced_states, weight_in_union, preferred_element_type=F32).reshape(
        own_rows * lax.axis_size("store"), union_count, BLOCK
    )
    picked = jnp.take_along_axis(dense_pre, slot_pos[:, :, None], axis=1)
    pre_act = lax.psum_scatter(
        (picked * all_keep[:, :, None].astype(F32)).reshape(
            own_rows * lax.axis_size("store"), slot_count * BLOCK
        ),
        "store",
        scatter_dimension=0,
        tiled=True,
    )
    own_ids = block_lists[:, 0, :]
    own_keep = jnp.any(own_ids[:, :, None] == union_ids[None, None, :], axis=-1)
    bias_rows = jnp.take(bias_blocks, jnp.maximum(own_ids, 0), axis=0).reshape(
        own_ids.shape[0], slot_count * BLOCK
    )
    active_mask = jnp.repeat(own_keep.astype(F32), BLOCK, axis=1)
    hidden = (jnp.maximum(pre_act + bias_rows, 0.0) * active_mask).astype(BF16)
    project_hidden = lax.all_gather(hidden, "store", axis=0, tiled=True)
    one_hot = jnp.logical_and(
        slot_pos[:, :, None] == union_range[None, None, :], all_keep[:, :, None]
    ).astype(BF16)
    spread = jnp.einsum(
        "rku,rkn->run",
        one_hot,
        project_hidden.reshape(-1, slot_count, BLOCK),
        preferred_element_type=F32,
    ).astype(BF16)
    partial_value = jnp.dot(
        spread.reshape(-1, union_count * BLOCK), weight_out_union, preferred_element_type=F32
    )
    row_terms = lax.all_to_all(partial_value, "store", split_axis=0, concat_axis=1, tiled=True)
    summed = lax.psum_scatter(row_terms, "tensor", scatter_dimension=1, tiled=True)
    return (summed + bias_out[None, :]).astype(BF16)


def solution(mesh):
    count = mesh.shape["store"]
    square = count == mesh.shape["tensor"] and count & (count - 1) == 0
    return jax.shard_map(
        fast if square else general,
        mesh=mesh,
        in_specs=(
            P(("groups", "store"), None),
            P("store", "tensor"),
            P("tensor"),
            P("tensor", "store"),
            P("tensor"),
            P(("groups", "store"), "tensor", None),
            P(("groups", "tensor"), None),
        ),
        out_specs=P(("groups", "store"), "tensor"),
        check_vma=False,
    )
```

```python
import functools

import jax
import jax.numpy as jnp
from jax import lax
from jax.experimental import pallas as pl
from jax.experimental.pallas import tpu as pltpu
from jax.sharding import PartitionSpec as P

BLOCK = 128
BF16 = jnp.bfloat16
F32 = jnp.float32
VMEM = pltpu.VMEM
SMEM = pltpu.SMEM


def whole(space):
    return pl.BlockSpec(memory_space=space)


def split_kernel(count, width, states_ref, ids_ref, union_ref, *refs):
    out_refs, union_out, ids, sems = refs[:count], refs[count], refs[count + 1], refs[count + 2]
    me = lax.axis_index("store")
    ids_copy = pltpu.make_async_copy(ids_ref, ids, sems.at[count])
    ids_copy.start()
    copies = []
    for k in list(range(1, count)) + [0]:
        start = pl.multiple_of((me ^ k) * width, BLOCK)
        copies.append(
            pltpu.make_async_copy(
                states_ref.at[:, pl.ds(start, width)], out_refs[k].at[:, :width], sems.at[k]
            )
        )
        copies[-1].start()
    copies.append(pltpu.make_async_copy(union_ref, union_out, sems.at[count + 1]))
    copies[-1].start()
    slots, rows = ids_ref.shape
    ids_copy.wait()
    padded = jnp.concatenate(
        [ids[...].astype(F32), jnp.full((BLOCK - slots, rows), -1.0, F32)], axis=0
    )
    tail = padded.T.astype(BF16)
    for k in range(count):
        out_refs[k][:, width:] = tail
    for copy in copies:
        copy.wait()


def gather_kernel(by_column, union_ref, weight_ref, out_ref, sems):
    copies = []
    for u in range(union_ref.shape[0]):
        block = pl.ds(pl.multiple_of(union_ref[u] * BLOCK, BLOCK), BLOCK)
        place = pl.ds(u * BLOCK, BLOCK)
        if by_column:
            source, target = weight_ref.at[:, block], out_ref.at[:, place]
        else:
            source, target = weight_ref.at[block, :], out_ref.at[place, :]
        copies.append(pltpu.make_async_copy(source, target, sems.at[u]))
        copies[-1].start()
    for copy in copies:
        copy.wait()


def gather(by_column, union_ids, weight, name):
    union = union_ids.shape[0]
    shape = (weight.shape[0], union * BLOCK) if by_column else (union * BLOCK, weight.shape[1])
    return pl.pallas_call(
        functools.partial(gather_kernel, by_column),
        out_shape=VMEM(shape, BF16),
        in_specs=[whole(SMEM), whole(pltpu.HBM)],
        out_specs=whole(VMEM),
        scratch_shapes=[pltpu.SemaphoreType.DMA((union,))],
        compiler_params=pltpu.CompilerParams(vmem_limit_bytes=40 * 2**20),
        cost_estimate=pl.CostEstimate(flops=0, bytes_accessed=4 * shape[0] * shape[1], transcendentals=0),
        name=name,
    )(union_ids, weight)


def first_kernel(count, slots, union_ref, *refs):
    chunk_refs = refs[:count][::-1]
    win_ref, pre_ref, ids_ref, dense = refs[count:]
    width, total = win_ref.shape
    rows = chunk_refs[0].shape[0]
    union = union_ref.shape[0]
    states = jnp.concatenate([c[:, :width] for c in chunk_refs], axis=0)
    ids = jnp.concatenate([c[:, width:] for c in chunk_refs], axis=0).astype(F32)
    ids_ref[...] = ids
    step = 2 * BLOCK
    for n in range(0, total, step):
        dense[:, n : n + step] = jnp.dot(states, win_ref[:, n : n + step], preferred_element_type=F32)
    for j in range(count):
        part = slice(j * rows, (j + 1) * rows)
        for k in range(slots):
            mine = jnp.broadcast_to(ids[part, k : k + 1], (rows, BLOCK))
            picked = jnp.zeros((rows, BLOCK), F32)
            for u in range(union):
                block = union_ref[u].astype(F32)
                picked = jnp.where(mine == block, dense[part, u * BLOCK : (u + 1) * BLOCK], picked)
            pre_ref[part, k * BLOCK : (k + 1) * BLOCK] = picked.astype(pre_ref.dtype)


def second_kernel(count, slots, union_ref, ids_ref, bias_ref, *refs):
    part_refs = refs[:count][::-1]
    wout_ref = refs[count]
    keep_ref, send_ref, spread, terms = refs[count + 1 :]
    store, tensor = lax.axis_index("store"), lax.axis_index("tensor")
    rows = ids_ref.shape[0] // count
    union = union_ref.shape[0]
    ids = ids_ref[...]
    for j in range(count):
        part = slice(j * rows, (j + 1) * rows)
        mines = [jnp.broadcast_to(ids[part, k : k + 1], (rows, BLOCK)) for k in range(slots)]
        pres = []
        for k in range(slots):
            cols = slice(k * BLOCK, (k + 1) * BLOCK)
            pres.append(
                sum(
                    p[(j ^ i) * rows : ((j ^ i) + 1) * rows, cols].astype(F32)
                    for i, p in enumerate(part_refs)
                )
            )
        for u in range(union):
            block = union_ref[u].astype(F32)
            value = jnp.zeros((rows, BLOCK), F32)
            bias = bias_ref[pl.ds(union_ref[u], 1), :]
            for k in range(slots):
                value = jnp.where(mines[k] == block, jnp.maximum(pres[k] + bias, 0.0), value)
            spread[part, u * BLOCK : (u + 1) * BLOCK] = value.astype(BF16)
    step = 2 * BLOCK
    width = wout_ref.shape[1]
    hidden = spread[...]
    for n in range(0, width, step):
        product = jnp.dot(hidden, wout_ref[:, n : n + step], preferred_element_type=F32)
        terms[:, :, n : n + step] = product.reshape(count, rows, step)
    chip, core = tensor // 2, tensor % 2
    for k in range(count // 2):
        part = slice(k * rows, (k + 1) * rows)
        keep_ref[part, :] = terms[store ^ (2 * core + (chip ^ k))]
        send_ref[part, :] = terms[store ^ (2 * (1 - core) + (chip ^ k))]


def fast(states, weight_in, bias_in, weight_out, bias_out, block_lists, union_blocks):
    count = lax.axis_size("store")
    width = weight_in.shape[0]
    rows = states.shape[0]
    slots = block_lists.shape[2]
    union = union_blocks.shape[1]
    total = union * BLOCK

    *chunks, union_ids = pl.pallas_call(
        functools.partial(split_kernel, count, width),
        out_shape=[VMEM((rows, width + BLOCK), BF16)] * count + [VMEM(union_blocks.shape, jnp.int32)],
        in_specs=[whole(pltpu.HBM)] * 3,
        out_specs=[whole(VMEM)] * (count + 1),
        scratch_shapes=[VMEM((slots, rows), jnp.int32), pltpu.SemaphoreType.DMA((count + 2,))],
        name="split_states",
    )(states, jnp.transpose(block_lists, (1, 2, 0))[0], union_blocks)
    union_ids = union_ids[0]

    def over_store(k):
        return [(i, i ^ k) for i in range(count)]

    far_first = list(range(count - 1, 0, -1))
    got = {k: lax.ppermute(chunks[k], "store", over_store(k)) for k in far_first}
    got = [got[k] for k in far_first] + [chunks[0]]

    win = gather(True, union_ids, weight_in, "gather_in")

    pre, ids = pl.pallas_call(
        functools.partial(first_kernel, count, slots),
        out_shape=[
            jax.ShapeDtypeStruct((count * rows, slots * BLOCK), BF16),
            jax.ShapeDtypeStruct((count * rows, BLOCK), F32),
        ],
        in_specs=[whole(SMEM)] + [whole(VMEM)] * (count + 1),
        out_specs=[whole(VMEM)] * 2,
        scratch_shapes=[VMEM((count * rows, total), F32)],
        compiler_params=pltpu.CompilerParams(vmem_limit_bytes=40 * 2**20),
        name="first_dot",
    )(union_ids, *got, win)

    parts = {k: lax.ppermute(pre, "store", over_store(k)) for k in far_first}
    parts = [parts[k] for k in far_first] + [pre]

    wout = gather(False, union_ids, weight_out, "gather_out")

    keep, send = pl.pallas_call(
        functools.partial(second_kernel, count, slots),
        out_shape=[VMEM((count // 2 * rows, width), F32)] * 2,
        in_specs=[whole(SMEM)] + [whole(VMEM)] * (count + 3),
        out_specs=[whole(VMEM)] * 2,
        scratch_shapes=[VMEM((count * rows, total), BF16), VMEM((count, rows, width), F32)],
        compiler_params=pltpu.CompilerParams(vmem_limit_bytes=40 * 2**20),
        name="second_dot",
    )(union_ids, ids, bias_in.reshape(-1, BLOCK), *parts, wout)

    pair = [(i, i ^ 1) for i in range(count)]
    both = (keep + lax.ppermute(send, "tensor", pair)).astype(BF16)

    def home(k):
        return [
            (z * count + 2 * x + c, (2 * c + (x ^ k)) * count + z)
            for z in range(count) for x in range(count // 2) for c in range(2)
        ]

    summed = sum(
        lax.ppermute(both[k * rows : (k + 1) * rows], ("store", "tensor"), home(k)).astype(F32)
        for k in range(count // 2)
    )
    return (summed + bias_out[None, :]).astype(BF16)


def general(states, weight_in, bias_in, weight_out, bias_out, block_lists, union_blocks):
    slice_width = weight_in.shape[0]
    union_ids = union_blocks[0]
    union_count = union_ids.shape[0]
    block_count = weight_in.shape[1] // BLOCK
    slot_count = block_lists.shape[2]
    own_rows = states.shape[0]
    sliced_states = lax.all_to_all(states, "store", split_axis=1, concat_axis=0, tiled=True)
    all_ids = lax.all_gather(block_lists, "store", axis=0, tiled=True)[:, 0, :]
    union_range = jnp.arange(union_count, dtype=jnp.int32)
    all_match = all_ids[:, :, None] == union_ids[None, None, :]
    all_keep = jnp.any(all_match, axis=-1)
    slot_pos = jnp.sum(jnp.where(all_match, union_range[None, None, :], 0), axis=-1)
    weight_in_union = jnp.take(
        weight_in.reshape(slice_width, block_count, BLOCK), union_ids, axis=1
    ).reshape(slice_width, union_count * BLOCK)
    weight_out_union = jnp.take(
        weight_out.reshape(block_count, BLOCK, slice_width), union_ids, axis=0
    ).reshape(union_count * BLOCK, slice_width)
    bias_blocks = bias_in.reshape(block_count, BLOCK)
    dense_pre = jnp.dot(sliced_states, weight_in_union, preferred_element_type=F32).reshape(
        own_rows * lax.axis_size("store"), union_count, BLOCK
    )
    picked = jnp.take_along_axis(dense_pre, slot_pos[:, :, None], axis=1)
    pre_act = lax.psum_scatter(
        (picked * all_keep[:, :, None].astype(F32)).reshape(
            own_rows * lax.axis_size("store"), slot_count * BLOCK
        ),
        "store",
        scatter_dimension=0,
        tiled=True,
    )
    own_ids = block_lists[:, 0, :]
    own_keep = jnp.any(own_ids[:, :, None] == union_ids[None, None, :], axis=-1)
    bias_rows = jnp.take(bias_blocks, jnp.maximum(own_ids, 0), axis=0).reshape(
        own_ids.shape[0], slot_count * BLOCK
    )
    active_mask = jnp.repeat(own_keep.astype(F32), BLOCK, axis=1)
    hidden = (jnp.maximum(pre_act + bias_rows, 0.0) * active_mask).astype(BF16)
    project_hidden = lax.all_gather(hidden, "store", axis=0, tiled=True)
    one_hot = jnp.logical_and(
        slot_pos[:, :, None] == union_range[None, None, :], all_keep[:, :, None]
    ).astype(BF16)
    spread = jnp.einsum(
        "rku,rkn->run",
        one_hot,
        project_hidden.reshape(-1, slot_count, BLOCK),
        preferred_element_type=F32,
    ).astype(BF16)
    partial_value = jnp.dot(
        spread.reshape(-1, union_count * BLOCK), weight_out_union, preferred_element_type=F32
    )
    row_terms = lax.all_to_all(partial_value, "store", split_axis=0, concat_axis=1, tiled=True)
    summed = lax.psum_scatter(row_terms, "tensor", scatter_dimension=1, tiled=True)
    return (summed + bias_out[None, :]).astype(BF16)


def solution(mesh):
    count = mesh.shape["store"]
    square = count == mesh.shape["tensor"] and count & (count - 1) == 0
    return jax.shard_map(
        fast if square else general,
        mesh=mesh,
        in_specs=(
            P(("groups", "store"), None),
            P("store", "tensor"),
            P("tensor"),
            P("tensor", "store"),
            P("tensor"),
            P(("groups", "store"), "tensor", None),
            P(("groups", "tensor"), None),
        ),
        out_specs=P(("groups", "store"), "tensor"),
        check_vma=False,
    )
```

```python
import functools

import jax
import jax.numpy as jnp
from jax import lax
from jax.experimental import pallas as pl
from jax.experimental.pallas import tpu as pltpu
from jax.sharding import PartitionSpec as P

BLOCK = 128
BF16 = jnp.bfloat16
F32 = jnp.float32
VMEM = pltpu.VMEM
SMEM = pltpu.SMEM


ORDER = (2, 3, 1)


def by_partner(refs):
    return [refs[(ORDER + (0,)).index(k)] for k in range(len(refs))]


def whole(space):
    return pl.BlockSpec(memory_space=space)


def split_kernel(count, width, states_ref, ids_ref, union_ref, *refs):
    out_refs, union_out, ids, sems = refs[:count], refs[count], refs[count + 1], refs[count + 2]
    me = lax.axis_index("store")
    ids_copy = pltpu.make_async_copy(ids_ref, ids, sems.at[count])
    ids_copy.start()
    copies = []
    for k in list(range(1, count)) + [0]:
        start = pl.multiple_of((me ^ k) * width, BLOCK)
        copies.append(
            pltpu.make_async_copy(
                states_ref.at[:, pl.ds(start, width)], out_refs[k].at[:, :width], sems.at[k]
            )
        )
        copies[-1].start()
    copies.append(pltpu.make_async_copy(union_ref, union_out, sems.at[count + 1]))
    copies[-1].start()
    slots, rows = ids_ref.shape
    ids_copy.wait()
    padded = jnp.concatenate(
        [ids[...].astype(F32), jnp.full((BLOCK - slots, rows), -1.0, F32)], axis=0
    )
    tail = padded.T.astype(BF16)
    for k in range(count):
        out_refs[k][:, width:] = tail
    for copy in copies:
        copy.wait()


def gather_kernel(by_column, union_ref, weight_ref, out_ref, sems):
    copies = []
    for u in range(union_ref.shape[0]):
        block = pl.ds(pl.multiple_of(union_ref[u] * BLOCK, BLOCK), BLOCK)
        place = pl.ds(u * BLOCK, BLOCK)
        if by_column:
            source, target = weight_ref.at[:, block], out_ref.at[:, place]
        else:
            source, target = weight_ref.at[block, :], out_ref.at[place, :]
        copies.append(pltpu.make_async_copy(source, target, sems.at[u]))
        copies[-1].start()
    for copy in copies:
        copy.wait()


def gather(by_column, union_ids, weight, name):
    union = union_ids.shape[0]
    shape = (weight.shape[0], union * BLOCK) if by_column else (union * BLOCK, weight.shape[1])
    return pl.pallas_call(
        functools.partial(gather_kernel, by_column),
        out_shape=VMEM(shape, BF16),
        in_specs=[whole(SMEM), whole(pltpu.HBM)],
        out_specs=whole(VMEM),
        scratch_shapes=[pltpu.SemaphoreType.DMA((union,))],
        compiler_params=pltpu.CompilerParams(vmem_limit_bytes=40 * 2**20),
        cost_estimate=pl.CostEstimate(flops=0, bytes_accessed=4 * shape[0] * shape[1], transcendentals=0),
        name=name,
    )(union_ids, weight)


def first_kernel(count, slots, union_ref, *refs):
    chunk_refs = by_partner(refs[:count])
    win_ref, pre_ref, ids_ref, dense = refs[count:]
    width, total = win_ref.shape
    rows = chunk_refs[0].shape[0]
    union = union_ref.shape[0]
    states = jnp.concatenate([c[:, :width] for c in chunk_refs], axis=0)
    ids = jnp.concatenate([c[:, width:] for c in chunk_refs], axis=0).astype(F32)
    ids_ref[...] = ids
    step = 2 * BLOCK
    for n in range(0, total, step):
        dense[:, n : n + step] = jnp.dot(states, win_ref[:, n : n + step], preferred_element_type=F32)
    for j in range(count):
        part = slice(j * rows, (j + 1) * rows)
        for k in range(slots):
            mine = jnp.broadcast_to(ids[part, k : k + 1], (rows, BLOCK))
            picked = jnp.zeros((rows, BLOCK), F32)
            for u in range(union):
                block = union_ref[u].astype(F32)
                picked = jnp.where(mine == block, dense[part, u * BLOCK : (u + 1) * BLOCK], picked)
            pre_ref[part, k * BLOCK : (k + 1) * BLOCK] = picked.astype(pre_ref.dtype)


def second_kernel(count, slots, union_ref, ids_ref, bias_ref, *refs):
    part_refs = by_partner(refs[:count])
    wout_ref = refs[count]
    keep_ref, send_ref, spread, terms = refs[count + 1 :]
    store, tensor = lax.axis_index("store"), lax.axis_index("tensor")
    rows = ids_ref.shape[0] // count
    union = union_ref.shape[0]
    ids = ids_ref[...]
    for j in range(count):
        part = slice(j * rows, (j + 1) * rows)
        mines = [jnp.broadcast_to(ids[part, k : k + 1], (rows, BLOCK)) for k in range(slots)]
        pres = []
        for k in range(slots):
            cols = slice(k * BLOCK, (k + 1) * BLOCK)
            pres.append(
                sum(
                    p[(j ^ i) * rows : ((j ^ i) + 1) * rows, cols].astype(F32)
                    for i, p in enumerate(part_refs)
                )
            )
        for u in range(union):
            block = union_ref[u].astype(F32)
            value = jnp.zeros((rows, BLOCK), F32)
            bias = bias_ref[pl.ds(union_ref[u], 1), :]
            for k in range(slots):
                value = jnp.where(mines[k] == block, jnp.maximum(pres[k] + bias, 0.0), value)
            spread[part, u * BLOCK : (u + 1) * BLOCK] = value.astype(BF16)
    step = 2 * BLOCK
    width = wout_ref.shape[1]
    hidden = spread[...]
    for n in range(0, width, step):
        product = jnp.dot(hidden, wout_ref[:, n : n + step], preferred_element_type=F32)
        terms[:, :, n : n + step] = product.reshape(count, rows, step)
    for turn in range(2):
        part = slice(turn * rows, (turn + 1) * rows)
        keep_ref[part, :] = terms[store ^ way_home(store, tensor, turn)]
        send_ref[part, :] = terms[store ^ way_home(store, tensor ^ 1, turn)]


def way_home(store, tensor, turn):
    high, low = store >> 1, store & 1
    odd = tensor & 1
    far = odd * 3 * (1 - high) + (1 - odd) * (1 + low)
    near = odd * (2 * (1 - low) + high) + (1 - odd) * store
    far_now = ((tensor >> 1) ^ high) ^ turn
    return far_now * far + (1 - far_now) * near


def fast(states, weight_in, bias_in, weight_out, bias_out, block_lists, union_blocks):
    count = lax.axis_size("store")
    width = weight_in.shape[0]
    rows = states.shape[0]
    slots = block_lists.shape[2]
    union = union_blocks.shape[1]
    total = union * BLOCK

    *chunks, union_ids = pl.pallas_call(
        functools.partial(split_kernel, count, width),
        out_shape=[VMEM((rows, width + BLOCK), BF16)] * count + [VMEM(union_blocks.shape, jnp.int32)],
        in_specs=[whole(pltpu.HBM)] * 3,
        out_specs=[whole(VMEM)] * (count + 1),
        scratch_shapes=[VMEM((slots, rows), jnp.int32), pltpu.SemaphoreType.DMA((count + 2,))],
        name="split_states",
    )(states, jnp.transpose(block_lists, (1, 2, 0))[0], union_blocks)
    union_ids = union_ids[0]

    def over_store(k):
        return [(i, i ^ k) for i in range(count)]

    got = [lax.ppermute(chunks[k], "store", over_store(k)) for k in ORDER] + [chunks[0]]

    win = gather(True, union_ids, weight_in, "gather_in")

    pre, ids = pl.pallas_call(
        functools.partial(first_kernel, count, slots),
        out_shape=[
            jax.ShapeDtypeStruct((count * rows, slots * BLOCK), BF16),
            jax.ShapeDtypeStruct((count * rows, BLOCK), F32),
        ],
        in_specs=[whole(SMEM)] + [whole(VMEM)] * (count + 1),
        out_specs=[whole(VMEM)] * 2,
        scratch_shapes=[VMEM((count * rows, total), F32)],
        compiler_params=pltpu.CompilerParams(vmem_limit_bytes=40 * 2**20),
        name="first_dot",
    )(union_ids, *got, win)

    parts = [lax.ppermute(pre, "store", over_store(k)) for k in ORDER] + [pre]

    wout = gather(False, union_ids, weight_out, "gather_out")

    keep, send = pl.pallas_call(
        functools.partial(second_kernel, count, slots),
        out_shape=[VMEM((count // 2 * rows, width), F32)] * 2,
        in_specs=[whole(SMEM)] + [whole(VMEM)] * (count + 3),
        out_specs=[whole(VMEM)] * 2,
        scratch_shapes=[VMEM((count * rows, total), BF16), VMEM((count, rows, width), F32)],
        compiler_params=pltpu.CompilerParams(vmem_limit_bytes=40 * 2**20),
        name="second_dot",
    )(union_ids, ids, bias_in.reshape(-1, BLOCK), *parts, wout)

    pair = [(i, i ^ 1) for i in range(count)]
    both = (keep + lax.ppermute(send, "tensor", pair)).astype(BF16)

    def home(turn):
        return [
            (z * count + t, way_home(z, t, turn) * count + z)
            for z in range(count) for t in range(count)
        ]

    summed = sum(
        lax.ppermute(both[k * rows : (k + 1) * rows], ("store", "tensor"), home(k)).astype(F32)
        for k in range(count // 2)
    )
    return (summed + bias_out[None, :]).astype(BF16)


def general(states, weight_in, bias_in, weight_out, bias_out, block_lists, union_blocks):
    slice_width = weight_in.shape[0]
    union_ids = union_blocks[0]
    union_count = union_ids.shape[0]
    block_count = weight_in.shape[1] // BLOCK
    slot_count = block_lists.shape[2]
    own_rows = states.shape[0]
    sliced_states = lax.all_to_all(states, "store", split_axis=1, concat_axis=0, tiled=True)
    all_ids = lax.all_gather(block_lists, "store", axis=0, tiled=True)[:, 0, :]
    union_range = jnp.arange(union_count, dtype=jnp.int32)
    all_match = all_ids[:, :, None] == union_ids[None, None, :]
    all_keep = jnp.any(all_match, axis=-1)
    slot_pos = jnp.sum(jnp.where(all_match, union_range[None, None, :], 0), axis=-1)
    weight_in_union = jnp.take(
        weight_in.reshape(slice_width, block_count, BLOCK), union_ids, axis=1
    ).reshape(slice_width, union_count * BLOCK)
    weight_out_union = jnp.take(
        weight_out.reshape(block_count, BLOCK, slice_width), union_ids, axis=0
    ).reshape(union_count * BLOCK, slice_width)
    bias_blocks = bias_in.reshape(block_count, BLOCK)
    dense_pre = jnp.dot(sliced_states, weight_in_union, preferred_element_type=F32).reshape(
        own_rows * lax.axis_size("store"), union_count, BLOCK
    )
    picked = jnp.take_along_axis(dense_pre, slot_pos[:, :, None], axis=1)
    pre_act = lax.psum_scatter(
        (picked * all_keep[:, :, None].astype(F32)).reshape(
            own_rows * lax.axis_size("store"), slot_count * BLOCK
        ),
        "store",
        scatter_dimension=0,
        tiled=True,
    )
    own_ids = block_lists[:, 0, :]
    own_keep = jnp.any(own_ids[:, :, None] == union_ids[None, None, :], axis=-1)
    bias_rows = jnp.take(bias_blocks, jnp.maximum(own_ids, 0), axis=0).reshape(
        own_ids.shape[0], slot_count * BLOCK
    )
    active_mask = jnp.repeat(own_keep.astype(F32), BLOCK, axis=1)
    hidden = (jnp.maximum(pre_act + bias_rows, 0.0) * active_mask).astype(BF16)
    project_hidden = lax.all_gather(hidden, "store", axis=0, tiled=True)
    one_hot = jnp.logical_and(
        slot_pos[:, :, None] == union_range[None, None, :], all_keep[:, :, None]
    ).astype(BF16)
    spread = jnp.einsum(
        "rku,rkn->run",
        one_hot,
        project_hidden.reshape(-1, slot_count, BLOCK),
        preferred_element_type=F32,
    ).astype(BF16)
    partial_value = jnp.dot(
        spread.reshape(-1, union_count * BLOCK), weight_out_union, preferred_element_type=F32
    )
    row_terms = lax.all_to_all(partial_value, "store", split_axis=0, concat_axis=1, tiled=True)
    summed = lax.psum_scatter(row_terms, "tensor", scatter_dimension=1, tiled=True)
    return (summed + bias_out[None, :]).astype(BF16)


def solution(mesh):
    count = mesh.shape["store"]
    square = count == 4 and mesh.shape["tensor"] == 4
    return jax.shard_map(
        fast if square else general,
        mesh=mesh,
        in_specs=(
            P(("groups", "store"), None),
            P("store", "tensor"),
            P("tensor"),
            P("tensor", "store"),
            P("tensor"),
            P(("groups", "store"), "tensor", None),
            P(("groups", "tensor"), None),
        ),
        out_specs=P(("groups", "store"), "tensor"),
        check_vma=False,
    )
```

```python
import functools

import jax
import jax.numpy as jnp
from jax import lax
from jax.experimental import pallas as pl
from jax.experimental.pallas import tpu as pltpu
from jax.sharding import PartitionSpec as P

BLOCK = 128
BF16 = jnp.bfloat16
F32 = jnp.float32
VMEM = pltpu.VMEM
SMEM = pltpu.SMEM


ORDER = (2, 3, 1)
ORDER_TWO = (3, 1, 2)


def by_partner(refs, order=ORDER):
    return [refs[(order + (0,)).index(k)] for k in range(len(refs))]


def whole(space):
    return pl.BlockSpec(memory_space=space)


def split_kernel(count, width, states_ref, ids_ref, union_ref, *refs):
    out_refs, union_out, ids, sems = refs[:count], refs[count], refs[count + 1], refs[count + 2]
    me = lax.axis_index("store")
    ids_copy = pltpu.make_async_copy(ids_ref, ids, sems.at[count])
    ids_copy.start()
    copies = []
    for k in list(range(1, count)) + [0]:
        start = pl.multiple_of((me ^ k) * width, BLOCK)
        copies.append(
            pltpu.make_async_copy(
                states_ref.at[:, pl.ds(start, width)], out_refs[k].at[:, :width], sems.at[k]
            )
        )
        copies[-1].start()
    union_copy = pltpu.make_async_copy(union_ref, union_out, sems.at[count + 1])
    union_copy.start()
    slots, rows = ids_ref.shape
    ids_copy.wait()
    union_copy.wait()
    blocks, union = ids[...], union_out[...]
    places = jnp.full((slots, rows), -1.0, F32)
    for u in range(union.shape[1]):
        places = jnp.where(blocks == union[:, u : u + 1], float(u), places)
    padded = jnp.concatenate([places, jnp.full((BLOCK - slots, rows), -1.0, F32)], axis=0)
    tail = padded.T.astype(BF16)
    for k in range(count):
        out_refs[k][:, width:] = tail
    for copy in copies:
        copy.wait()


def gather_kernel(by_column, union_ref, weight_ref, *refs):
    *bias_refs, sems = refs
    out_ref = bias_refs.pop(len(bias_refs) // 2)
    union = union_ref.shape[0]
    copies = []
    for u in range(union):
        block = pl.ds(pl.multiple_of(union_ref[u] * BLOCK, BLOCK), BLOCK)
        place = pl.ds(u * BLOCK, BLOCK)
        if by_column:
            source, target = weight_ref.at[:, block], out_ref.at[:, place]
        else:
            source, target = weight_ref.at[block, :], out_ref.at[place, :]
        copies.append(pltpu.make_async_copy(source, target, sems.at[u]))
        copies[-1].start()
    if bias_refs:
        bias_ref, bias_out = bias_refs
        for u in range(union):
            bias_out[u : u + 1, :] = bias_ref[pl.ds(union_ref[u], 1), :]
    for copy in copies:
        copy.wait()


def gather(by_column, union_ids, weight, name, *bias):
    union = union_ids.shape[0]
    shape = (weight.shape[0], union * BLOCK) if by_column else (union * BLOCK, weight.shape[1])
    return pl.pallas_call(
        functools.partial(gather_kernel, by_column),
        out_shape=[VMEM(shape, BF16)] + [VMEM((union, BLOCK), F32)] * len(bias),
        in_specs=[whole(SMEM), whole(pltpu.HBM)] + [whole(VMEM)] * len(bias),
        out_specs=[whole(VMEM)] * (1 + len(bias)),
        scratch_shapes=[pltpu.SemaphoreType.DMA((union,))],
        compiler_params=pltpu.CompilerParams(vmem_limit_bytes=40 * 2**20),
        cost_estimate=pl.CostEstimate(flops=0, bytes_accessed=4 * shape[0] * shape[1], transcendentals=0),
        name=name,
    )(union_ids, weight, *bias)


def first_kernel(count, slots, *refs):
    chunk_refs = by_partner(refs[:count])
    win_ref, pre_ref, ids_ref, dense = refs[count:]
    width, total = win_ref.shape
    rows = chunk_refs[0].shape[0]
    union = total // BLOCK
    states = jnp.concatenate([c[:, :width] for c in chunk_refs], axis=0)
    ids = jnp.concatenate([c[:, width:] for c in chunk_refs], axis=0).astype(F32)
    ids_ref[...] = ids
    step = 2 * BLOCK
    for n in range(0, total, step):
        dense[:, n : n + step] = jnp.dot(states, win_ref[:, n : n + step], preferred_element_type=F32)
    for j in range(count):
        part = slice(j * rows, (j + 1) * rows)
        for k in range(slots):
            mine = jnp.broadcast_to(ids[part, k : k + 1], (rows, BLOCK))
            picked = jnp.zeros((rows, BLOCK), F32)
            for u in range(union):
                picked = jnp.where(mine == float(u), dense[part, u * BLOCK : (u + 1) * BLOCK], picked)
            pre_ref[part, k * BLOCK : (k + 1) * BLOCK] = picked.astype(pre_ref.dtype)


def second_kernel(count, slots, ids_ref, bias_ref, *refs):
    part_refs = by_partner(refs[:count], ORDER_TWO)
    wout_ref = refs[count]
    keep_ref, send_ref, spread, terms = refs[count + 1 :]
    store, tensor = lax.axis_index("store"), lax.axis_index("tensor")
    rows = ids_ref.shape[0] // count
    union = bias_ref.shape[0]
    ids = ids_ref[...]
    for j in range(count):
        part = slice(j * rows, (j + 1) * rows)
        mines = [jnp.broadcast_to(ids[part, k : k + 1], (rows, BLOCK)) for k in range(slots)]
        pres = []
        for k in range(slots):
            cols = slice(k * BLOCK, (k + 1) * BLOCK)
            pres.append(
                sum(
                    p[(j ^ i) * rows : ((j ^ i) + 1) * rows, cols].astype(F32)
                    for i, p in enumerate(part_refs)
                )
            )
        for u in range(union):
            value = jnp.zeros((rows, BLOCK), F32)
            bias = bias_ref[u : u + 1, :]
            for k in range(slots):
                value = jnp.where(mines[k] == float(u), jnp.maximum(pres[k] + bias, 0.0), value)
            spread[part, u * BLOCK : (u + 1) * BLOCK] = value.astype(BF16)
    step = 2 * BLOCK
    width = wout_ref.shape[1]
    hidden = spread[...]
    for n in range(0, width, step):
        product = jnp.dot(hidden, wout_ref[:, n : n + step], preferred_element_type=F32)
        terms[:, :, n : n + step] = product.reshape(count, rows, step)
    for turn in range(2):
        part = slice(turn * rows, (turn + 1) * rows)
        keep_ref[part, :] = terms[store ^ way_home(store, tensor, turn)]
        send_ref[part, :] = terms[store ^ way_home(store, tensor ^ 1, turn)]


WAY_HOME = (
    ((2, 1), (3, 0), (1, 2), (0, 3)),
    ((1, 3), (2, 0), (3, 1), (0, 2)),
    ((2, 3), (0, 1), (3, 2), (1, 0)),
    ((3, 2), (0, 1), (2, 3), (1, 0)),
)


def way_home(store, tensor, turn):
    code = sum(
        WAY_HOME[s][t][turn] << 2 * (4 * s + t) for s in range(4) for t in range(4)
    )
    code = jnp.int32(code - (1 << 32) if code >= 1 << 31 else code)
    return lax.shift_right_logical(code, 2 * (4 * store + tensor)) & 3


def fast(states, weight_in, bias_in, weight_out, bias_out, block_lists, union_blocks):
    count = lax.axis_size("store")
    width = weight_in.shape[0]
    rows = states.shape[0]
    slots = block_lists.shape[2]
    union = union_blocks.shape[1]
    total = union * BLOCK

    *chunks, union_ids = pl.pallas_call(
        functools.partial(split_kernel, count, width),
        out_shape=[VMEM((rows, width + BLOCK), BF16)] * count + [VMEM(union_blocks.shape, jnp.int32)],
        in_specs=[whole(pltpu.HBM)] * 3,
        out_specs=[whole(VMEM)] * (count + 1),
        scratch_shapes=[VMEM((slots, rows), jnp.int32), pltpu.SemaphoreType.DMA((count + 2,))],
        name="split_states",
    )(states, jnp.transpose(block_lists, (1, 2, 0))[0], union_blocks)
    union_ids = union_ids[0]

    def over_store(k):
        return [(i, i ^ k) for i in range(count)]

    got = [lax.ppermute(chunks[k], "store", over_store(k)) for k in ORDER] + [chunks[0]]

    (win,) = gather(True, union_ids, weight_in, "gather_in")

    pre, ids = pl.pallas_call(
        functools.partial(first_kernel, count, slots),
        out_shape=[
            jax.ShapeDtypeStruct((count * rows, slots * BLOCK), BF16),
            jax.ShapeDtypeStruct((count * rows, BLOCK), F32),
        ],
        in_specs=[whole(VMEM)] * (count + 1),
        out_specs=[whole(VMEM)] * 2,
        scratch_shapes=[VMEM((count * rows, total), F32)],
        compiler_params=pltpu.CompilerParams(vmem_limit_bytes=40 * 2**20),
        name="first_dot",
    )(*got, win)

    parts = [lax.ppermute(pre, "store", over_store(k)) for k in ORDER_TWO] + [pre]

    wout, bias = gather(False, union_ids, weight_out, "gather_out", bias_in.reshape(-1, BLOCK))

    keep, send = pl.pallas_call(
        functools.partial(second_kernel, count, slots),
        out_shape=[VMEM((count // 2 * rows, width), F32)] * 2,
        in_specs=[whole(VMEM)] * (count + 3),
        out_specs=[whole(VMEM)] * 2,
        scratch_shapes=[VMEM((count * rows, total), BF16), VMEM((count, rows, width), F32)],
        compiler_params=pltpu.CompilerParams(vmem_limit_bytes=40 * 2**20),
        name="second_dot",
    )(ids, bias, *parts, wout)

    pair = [(i, i ^ 1) for i in range(count)]
    both = (keep + lax.ppermute(send, "tensor", pair)).astype(BF16)

    def home(turn):
        return [
            (z * count + t, WAY_HOME[z][t][turn] * count + z)
            for z in range(count) for t in range(count)
        ]

    summed = sum(
        lax.ppermute(both[k * rows : (k + 1) * rows], ("store", "tensor"), home(k)).astype(F32)
        for k in range(count // 2)
    )
    return (summed + bias_out[None, :]).astype(BF16)


def general(states, weight_in, bias_in, weight_out, bias_out, block_lists, union_blocks):
    slice_width = weight_in.shape[0]
    union_ids = union_blocks[0]
    union_count = union_ids.shape[0]
    block_count = weight_in.shape[1] // BLOCK
    slot_count = block_lists.shape[2]
    own_rows = states.shape[0]
    sliced_states = lax.all_to_all(states, "store", split_axis=1, concat_axis=0, tiled=True)
    all_ids = lax.all_gather(block_lists, "store", axis=0, tiled=True)[:, 0, :]
    union_range = jnp.arange(union_count, dtype=jnp.int32)
    all_match = all_ids[:, :, None] == union_ids[None, None, :]
    all_keep = jnp.any(all_match, axis=-1)
    slot_pos = jnp.sum(jnp.where(all_match, union_range[None, None, :], 0), axis=-1)
    weight_in_union = jnp.take(
        weight_in.reshape(slice_width, block_count, BLOCK), union_ids, axis=1
    ).reshape(slice_width, union_count * BLOCK)
    weight_out_union = jnp.take(
        weight_out.reshape(block_count, BLOCK, slice_width), union_ids, axis=0
    ).reshape(union_count * BLOCK, slice_width)
    bias_blocks = bias_in.reshape(block_count, BLOCK)
    dense_pre = jnp.dot(sliced_states, weight_in_union, preferred_element_type=F32).reshape(
        own_rows * lax.axis_size("store"), union_count, BLOCK
    )
    picked = jnp.take_along_axis(dense_pre, slot_pos[:, :, None], axis=1)
    pre_act = lax.psum_scatter(
        (picked * all_keep[:, :, None].astype(F32)).reshape(
            own_rows * lax.axis_size("store"), slot_count * BLOCK
        ),
        "store",
        scatter_dimension=0,
        tiled=True,
    )
    own_ids = block_lists[:, 0, :]
    own_keep = jnp.any(own_ids[:, :, None] == union_ids[None, None, :], axis=-1)
    bias_rows = jnp.take(bias_blocks, jnp.maximum(own_ids, 0), axis=0).reshape(
        own_ids.shape[0], slot_count * BLOCK
    )
    active_mask = jnp.repeat(own_keep.astype(F32), BLOCK, axis=1)
    hidden = (jnp.maximum(pre_act + bias_rows, 0.0) * active_mask).astype(BF16)
    project_hidden = lax.all_gather(hidden, "store", axis=0, tiled=True)
    one_hot = jnp.logical_and(
        slot_pos[:, :, None] == union_range[None, None, :], all_keep[:, :, None]
    ).astype(BF16)
    spread = jnp.einsum(
        "rku,rkn->run",
        one_hot,
        project_hidden.reshape(-1, slot_count, BLOCK),
        preferred_element_type=F32,
    ).astype(BF16)
    partial_value = jnp.dot(
        spread.reshape(-1, union_count * BLOCK), weight_out_union, preferred_element_type=F32
    )
    row_terms = lax.all_to_all(partial_value, "store", split_axis=0, concat_axis=1, tiled=True)
    summed = lax.psum_scatter(row_terms, "tensor", scatter_dimension=1, tiled=True)
    return (summed + bias_out[None, :]).astype(BF16)


def solution(mesh):
    count = mesh.shape["store"]
    square = count == 4 and mesh.shape["tensor"] == 4
    return jax.shard_map(
        fast if square else general,
        mesh=mesh,
        in_specs=(
            P(("groups", "store"), None),
            P("store", "tensor"),
            P("tensor"),
            P("tensor", "store"),
            P("tensor"),
            P(("groups", "store"), "tensor", None),
            P(("groups", "tensor"), None),
        ),
        out_specs=P(("groups", "store"), "tensor"),
        check_vma=False,
    )
```

```python
import functools

import jax
import jax.numpy as jnp
from jax import lax
from jax.experimental import pallas as pl
from jax.experimental.pallas import tpu as pltpu
from jax.sharding import PartitionSpec as P

BLOCK = 128
BF16 = jnp.bfloat16
F32 = jnp.float32
VMEM = pltpu.VMEM
SMEM = pltpu.SMEM


ORDER = (2, 3, 1)
ORDER_TWO = (3, 1, 2)


def by_partner(refs, order=ORDER):
    return [refs[(order + (0,)).index(k)] for k in range(len(refs))]


def whole(space):
    return pl.BlockSpec(memory_space=space)


def split_kernel(count, width, states_ref, ids_ref, union_ref, *refs):
    out_refs, union_out, ids, sems = refs[:count], refs[count], refs[count + 1], refs[count + 2]
    me = lax.axis_index("store")
    ids_copy = pltpu.make_async_copy(ids_ref, ids, sems.at[count])
    ids_copy.start()
    copies = []
    for k in list(range(1, count)) + [0]:
        start = pl.multiple_of((me ^ k) * width, BLOCK)
        copies.append(
            pltpu.make_async_copy(
                states_ref.at[:, pl.ds(start, width)], out_refs[k].at[:, :width], sems.at[k]
            )
        )
        copies[-1].start()
    union_copy = pltpu.make_async_copy(union_ref, union_out, sems.at[count + 1])
    union_copy.start()
    slots, rows = ids_ref.shape
    ids_copy.wait()
    union_copy.wait()
    blocks, union = ids[...], union_out[...]
    places = jnp.full((slots, rows), -1.0, F32)
    for u in range(union.shape[1]):
        places = jnp.where(blocks == union[:, u : u + 1], float(u), places)
    padded = jnp.concatenate([places, jnp.full((BLOCK - slots, rows), -1.0, F32)], axis=0)
    tail = padded.T.astype(BF16)
    for k in range(count):
        out_refs[k][:, width:] = tail
    for copy in copies:
        copy.wait()


def gather_kernel(by_column, union_ref, weight_ref, *refs):
    *bias_refs, sems = refs
    out_ref = bias_refs.pop(len(bias_refs) // 2)
    union = union_ref.shape[0]
    copies = []
    for u in range(union):
        block = pl.ds(pl.multiple_of(union_ref[u] * BLOCK, BLOCK), BLOCK)
        place = pl.ds(u * BLOCK, BLOCK)
        if by_column:
            source, target = weight_ref.at[:, block], out_ref.at[:, place]
        else:
            source, target = weight_ref.at[block, :], out_ref.at[place, :]
        copies.append(pltpu.make_async_copy(source, target, sems.at[u]))
        copies[-1].start()
    if bias_refs:
        bias_ref, bias_out = bias_refs
        for u in range(union):
            bias_out[u : u + 1, :] = bias_ref[pl.ds(union_ref[u], 1), :]
    for copy in copies:
        copy.wait()


def gather(by_column, union_ids, weight, name, *bias):
    union = union_ids.shape[0]
    shape = (weight.shape[0], union * BLOCK) if by_column else (union * BLOCK, weight.shape[1])
    return pl.pallas_call(
        functools.partial(gather_kernel, by_column),
        out_shape=[VMEM(shape, BF16)] + [VMEM((union, BLOCK), F32)] * len(bias),
        in_specs=[whole(SMEM), whole(pltpu.HBM)] + [whole(VMEM)] * len(bias),
        out_specs=[whole(VMEM)] * (1 + len(bias)),
        scratch_shapes=[pltpu.SemaphoreType.DMA((union,))],
        compiler_params=pltpu.CompilerParams(vmem_limit_bytes=40 * 2**20),
        cost_estimate=pl.CostEstimate(flops=0, bytes_accessed=4 * shape[0] * shape[1], transcendentals=0),
        name=name,
    )(union_ids, weight, *bias)


def first_kernel(count, slots, *refs):
    chunk_refs = by_partner(refs[:count])
    win_ref, pre_ref, ids_ref, dense = refs[count:]
    width, total = win_ref.shape
    rows = chunk_refs[0].shape[0]
    union = total // BLOCK
    states = jnp.concatenate([c[:, :width] for c in chunk_refs], axis=0)
    ids = jnp.concatenate([c[:, width:] for c in chunk_refs], axis=0).astype(F32)
    ids_ref[...] = ids
    step = 2 * BLOCK
    for n in range(0, total, step):
        dense[:, n : n + step] = jnp.dot(states, win_ref[:, n : n + step], preferred_element_type=F32)
    for j in range(count):
        part = slice(j * rows, (j + 1) * rows)
        for k in range(slots):
            mine = jnp.broadcast_to(ids[part, k : k + 1], (rows, BLOCK))
            picked = jnp.zeros((rows, BLOCK), F32)
            for u in range(union):
                picked = jnp.where(mine == float(u), dense[part, u * BLOCK : (u + 1) * BLOCK], picked)
            pre_ref[part, k * BLOCK : (k + 1) * BLOCK] = picked.astype(pre_ref.dtype)


def second_kernel(count, slots, ids_ref, bias_ref, *refs):
    part_refs = by_partner(refs[:count], ORDER_TWO)
    wout_ref = refs[count]
    keep_ref, send_ref, spread, terms = refs[count + 1 :]
    store, tensor = lax.axis_index("store"), lax.axis_index("tensor")
    rows = ids_ref.shape[0] // count
    union = bias_ref.shape[0]
    ids = ids_ref[...]
    for j in range(count):
        part = slice(j * rows, (j + 1) * rows)
        mines = [jnp.broadcast_to(ids[part, k : k + 1], (rows, BLOCK)) for k in range(slots)]
        pres = []
        for k in range(slots):
            cols = slice(k * BLOCK, (k + 1) * BLOCK)
            pres.append(
                sum(
                    p[(j ^ i) * rows : ((j ^ i) + 1) * rows, cols].astype(F32)
                    for i, p in enumerate(part_refs)
                )
            )
        for u in range(union):
            value = jnp.zeros((rows, BLOCK), F32)
            bias = bias_ref[u : u + 1, :]
            for k in range(slots):
                value = jnp.where(mines[k] == float(u), jnp.maximum(pres[k] + bias, 0.0), value)
            spread[part, u * BLOCK : (u + 1) * BLOCK] = value.astype(BF16)
    step = 2 * BLOCK
    width = wout_ref.shape[1]
    hidden = spread[...]
    for n in range(0, width, step):
        product = jnp.dot(hidden, wout_ref[:, n : n + step], preferred_element_type=F32)
        terms[:, :, n : n + step] = product.reshape(count, rows, step)
    for turn in range(2):
        part = slice(turn * rows, (turn + 1) * rows)
        keep_ref[part, :] = terms[store ^ way_home(store, tensor, turn)]
        send_ref[part, :] = terms[store ^ way_home(store, tensor ^ 1, turn)]


WAY_HOME = (
    ((2, 1), (3, 0), (1, 2), (0, 3)),
    ((1, 3), (2, 0), (3, 1), (0, 2)),
    ((1, 0), (3, 2), (0, 1), (2, 3)),
    ((1, 3), (2, 0), (3, 1), (0, 2)),
)


def way_home(store, tensor, turn):
    code = sum(
        WAY_HOME[s][t][turn] << 2 * (4 * s + t) for s in range(4) for t in range(4)
    )
    code = jnp.int32(code - (1 << 32) if code >= 1 << 31 else code)
    return lax.shift_right_logical(code, 2 * (4 * store + tensor)) & 3


def fast(states, weight_in, bias_in, weight_out, bias_out, block_lists, union_blocks):
    count = lax.axis_size("store")
    width = weight_in.shape[0]
    rows = states.shape[0]
    slots = block_lists.shape[2]
    union = union_blocks.shape[1]
    total = union * BLOCK

    *chunks, union_ids = pl.pallas_call(
        functools.partial(split_kernel, count, width),
        out_shape=[VMEM((rows, width + BLOCK), BF16)] * count + [VMEM(union_blocks.shape, jnp.int32)],
        in_specs=[whole(pltpu.HBM)] * 3,
        out_specs=[whole(VMEM)] * (count + 1),
        scratch_shapes=[VMEM((slots, rows), jnp.int32), pltpu.SemaphoreType.DMA((count + 2,))],
        name="split_states",
    )(states, jnp.transpose(block_lists, (1, 2, 0))[0], union_blocks)
    union_ids = union_ids[0]

    def over_store(k):
        return [(i, i ^ k) for i in range(count)]

    got = [lax.ppermute(chunks[k], "store", over_store(k)) for k in ORDER] + [chunks[0]]

    (win,) = gather(True, union_ids, weight_in, "gather_in")

    pre, ids = pl.pallas_call(
        functools.partial(first_kernel, count, slots),
        out_shape=[
            jax.ShapeDtypeStruct((count * rows, slots * BLOCK), BF16),
            jax.ShapeDtypeStruct((count * rows, BLOCK), F32),
        ],
        in_specs=[whole(VMEM)] * (count + 1),
        out_specs=[whole(VMEM)] * 2,
        scratch_shapes=[VMEM((count * rows, total), F32)],
        compiler_params=pltpu.CompilerParams(vmem_limit_bytes=40 * 2**20),
        name="first_dot",
    )(*got, win)

    parts = [lax.ppermute(pre, "store", over_store(k)) for k in ORDER_TWO] + [pre]

    wout, bias = gather(False, union_ids, weight_out, "gather_out", bias_in.reshape(-1, BLOCK))

    keep, send = pl.pallas_call(
        functools.partial(second_kernel, count, slots),
        out_shape=[VMEM((count // 2 * rows, width), F32)] * 2,
        in_specs=[whole(VMEM)] * (count + 3),
        out_specs=[whole(VMEM)] * 2,
        scratch_shapes=[VMEM((count * rows, total), BF16), VMEM((count, rows, width), F32)],
        compiler_params=pltpu.CompilerParams(vmem_limit_bytes=40 * 2**20),
        name="second_dot",
    )(ids, bias, *parts, wout)

    pair = [(i, i ^ 1) for i in range(count)]
    both = (keep + lax.ppermute(send, "tensor", pair)).astype(BF16)

    def home(turn):
        return [
            (z * count + t, WAY_HOME[z][t][turn] * count + z)
            for z in range(count) for t in range(count)
        ]

    summed = sum(
        lax.ppermute(both[k * rows : (k + 1) * rows], ("store", "tensor"), home(k)).astype(F32)
        for k in range(count // 2)
    )
    return (summed + bias_out[None, :]).astype(BF16)


def general(states, weight_in, bias_in, weight_out, bias_out, block_lists, union_blocks):
    slice_width = weight_in.shape[0]
    union_ids = union_blocks[0]
    union_count = union_ids.shape[0]
    block_count = weight_in.shape[1] // BLOCK
    slot_count = block_lists.shape[2]
    own_rows = states.shape[0]
    sliced_states = lax.all_to_all(states, "store", split_axis=1, concat_axis=0, tiled=True)
    all_ids = lax.all_gather(block_lists, "store", axis=0, tiled=True)[:, 0, :]
    union_range = jnp.arange(union_count, dtype=jnp.int32)
    all_match = all_ids[:, :, None] == union_ids[None, None, :]
    all_keep = jnp.any(all_match, axis=-1)
    slot_pos = jnp.sum(jnp.where(all_match, union_range[None, None, :], 0), axis=-1)
    weight_in_union = jnp.take(
        weight_in.reshape(slice_width, block_count, BLOCK), union_ids, axis=1
    ).reshape(slice_width, union_count * BLOCK)
    weight_out_union = jnp.take(
        weight_out.reshape(block_count, BLOCK, slice_width), union_ids, axis=0
    ).reshape(union_count * BLOCK, slice_width)
    bias_blocks = bias_in.reshape(block_count, BLOCK)
    dense_pre = jnp.dot(sliced_states, weight_in_union, preferred_element_type=F32).reshape(
        own_rows * lax.axis_size("store"), union_count, BLOCK
    )
    picked = jnp.take_along_axis(dense_pre, slot_pos[:, :, None], axis=1)
    pre_act = lax.psum_scatter(
        (picked * all_keep[:, :, None].astype(F32)).reshape(
            own_rows * lax.axis_size("store"), slot_count * BLOCK
        ),
        "store",
        scatter_dimension=0,
        tiled=True,
    )
    own_ids = block_lists[:, 0, :]
    own_keep = jnp.any(own_ids[:, :, None] == union_ids[None, None, :], axis=-1)
    bias_rows = jnp.take(bias_blocks, jnp.maximum(own_ids, 0), axis=0).reshape(
        own_ids.shape[0], slot_count * BLOCK
    )
    active_mask = jnp.repeat(own_keep.astype(F32), BLOCK, axis=1)
    hidden = (jnp.maximum(pre_act + bias_rows, 0.0) * active_mask).astype(BF16)
    project_hidden = lax.all_gather(hidden, "store", axis=0, tiled=True)
    one_hot = jnp.logical_and(
        slot_pos[:, :, None] == union_range[None, None, :], all_keep[:, :, None]
    ).astype(BF16)
    spread = jnp.einsum(
        "rku,rkn->run",
        one_hot,
        project_hidden.reshape(-1, slot_count, BLOCK),
        preferred_element_type=F32,
    ).astype(BF16)
    partial_value = jnp.dot(
        spread.reshape(-1, union_count * BLOCK), weight_out_union, preferred_element_type=F32
    )
    row_terms = lax.all_to_all(partial_value, "store", split_axis=0, concat_axis=1, tiled=True)
    summed = lax.psum_scatter(row_terms, "tensor", scatter_dimension=1, tiled=True)
    return (summed + bias_out[None, :]).astype(BF16)


def solution(mesh):
    count = mesh.shape["store"]
    square = count == 4 and mesh.shape["tensor"] == 4
    return jax.shard_map(
        fast if square else general,
        mesh=mesh,
        in_specs=(
            P(("groups", "store"), None),
            P("store", "tensor"),
            P("tensor"),
            P("tensor", "store"),
            P("tensor"),
            P(("groups", "store"), "tensor", None),
            P(("groups", "tensor"), None),
        ),
        out_specs=P(("groups", "store"), "tensor"),
        check_vma=False,
    )
```

```python
import functools

import jax
import jax.numpy as jnp
from jax import lax
from jax.experimental import pallas as pl
from jax.experimental.pallas import tpu as pltpu
from jax.sharding import PartitionSpec as P

BLOCK = 128
BF16 = jnp.bfloat16
F32 = jnp.float32
VMEM = pltpu.VMEM


ROUND_ONE = ((2, 3, 1), (2, 3, 1))
ROUND_TWO = ((1, 2, 3), (3, 1, 2))


def partner(order, turn):
    odd = lax.axis_index("tensor") & 1
    return odd * order[1][turn] + (1 - odd) * order[0][turn]


def whole(space):
    return pl.BlockSpec(memory_space=space)


def split_kernel(count, width, states_ref, ids_ref, union_ref, *refs):
    out_refs, union_out, ids, sems = refs[:count], refs[count], refs[count + 1], refs[count + 2]
    me = lax.axis_index("store")
    ids_copy = pltpu.make_async_copy(ids_ref, ids, sems.at[count])
    ids_copy.start()
    copies = []
    for turn in range(count):
        other = me ^ partner(ROUND_ONE, turn) if turn < count - 1 else me
        start = pl.multiple_of(other * width, BLOCK)
        copies.append(
            pltpu.make_async_copy(
                states_ref.at[:, pl.ds(start, width)], out_refs[turn].at[:, :width], sems.at[turn]
            )
        )
        copies[-1].start()
    union_copy = pltpu.make_async_copy(union_ref, union_out, sems.at[count + 1])
    union_copy.start()
    slots, rows = ids_ref.shape
    ids_copy.wait()
    union_copy.wait()
    blocks, union = ids[...], union_out[...]
    places = jnp.full((slots, rows), -1.0, F32)
    for u in range(union.shape[1]):
        places = jnp.where(blocks == union[:, u : u + 1], float(u), places)
    padded = jnp.concatenate([places, jnp.full((BLOCK - slots, rows), -1.0, F32)], axis=0)
    tail = padded.T.astype(BF16)
    for k in range(count):
        out_refs[k][:, width:] = tail
    for copy in copies:
        copy.wait()


def gather_kernel(by_column, union_ref, weight_ref, *refs):
    *bias_refs, sems = refs
    out_ref = bias_refs.pop(len(bias_refs) // 2)
    union = union_ref.shape[1]
    copies = []
    for u in range(union):
        block = pl.ds(pl.multiple_of(union_ref[0, u] * BLOCK, BLOCK), BLOCK)
        place = pl.ds(u * BLOCK, BLOCK)
        if by_column:
            source, target = weight_ref.at[:, block], out_ref.at[:, place]
        else:
            source, target = weight_ref.at[block, :], out_ref.at[place, :]
        copies.append(pltpu.make_async_copy(source, target, sems.at[u]))
        copies[-1].start()
    if bias_refs:
        bias_ref, bias_out = bias_refs
        for u in range(union):
            bias_out[u : u + 1, :] = bias_ref[pl.ds(union_ref[0, u], 1), :]
    for copy in copies:
        copy.wait()


def gather(by_column, union_ids, weight, name, *bias):
    union = union_ids.shape[1]
    shape = (weight.shape[0], union * BLOCK) if by_column else (union * BLOCK, weight.shape[1])
    return pl.pallas_call(
        functools.partial(gather_kernel, by_column),
        out_shape=[VMEM(shape, BF16)] + [VMEM((union, BLOCK), F32)] * len(bias),
        in_specs=[whole(VMEM), whole(pltpu.HBM)] + [whole(VMEM)] * len(bias),
        out_specs=[whole(VMEM)] * (1 + len(bias)),
        scratch_shapes=[pltpu.SemaphoreType.DMA((union,))],
        compiler_params=pltpu.CompilerParams(vmem_limit_bytes=40 * 2**20),
        cost_estimate=pl.CostEstimate(flops=0, bytes_accessed=4 * shape[0] * shape[1], transcendentals=0),
        name=name,
    )(union_ids, weight, *bias)


def first_kernel(count, slots, *refs):
    chunk_refs = refs[:count]
    win_ref, pre_ref, ids_ref, dense, chunks = refs[count:]
    width, total = win_ref.shape
    rows = chunk_refs[0].shape[0]
    union = total // BLOCK
    for turn in range(count - 1):
        place = pl.multiple_of(partner(ROUND_ONE, turn) * rows, rows)
        chunks[pl.ds(place, rows), :] = chunk_refs[turn][...]
    chunks[:rows, :] = chunk_refs[count - 1][...]
    states = chunks[:, :width]
    ids = chunks[:, width:].astype(F32)
    ids_ref[...] = ids
    step = 2 * BLOCK
    for n in range(0, total, step):
        dense[:, n : n + step] = jnp.dot(states, win_ref[:, n : n + step], preferred_element_type=F32)
    for j in range(count):
        part = slice(j * rows, (j + 1) * rows)
        for k in range(slots):
            mine = jnp.broadcast_to(ids[part, k : k + 1], (rows, BLOCK))
            picked = jnp.zeros((rows, BLOCK), F32)
            for u in range(union):
                picked = jnp.where(mine == float(u), dense[part, u * BLOCK : (u + 1) * BLOCK], picked)
            pre_ref[part, k * BLOCK : (k + 1) * BLOCK] = picked.astype(pre_ref.dtype)


def second_kernel(count, slots, ids_ref, bias_ref, *refs):
    part_refs = refs[:count]
    partners = [partner(ROUND_TWO, turn) for turn in range(count - 1)] + [0]
    wout_ref = refs[count]
    keep_ref, send_ref, spread, terms = refs[count + 1 :]
    store, tensor = lax.axis_index("store"), lax.axis_index("tensor")
    rows = ids_ref.shape[0] // count
    union = bias_ref.shape[0]
    ids = ids_ref[...]
    for j in range(count):
        part = slice(j * rows, (j + 1) * rows)
        mines = [jnp.broadcast_to(ids[part, k : k + 1], (rows, BLOCK)) for k in range(slots)]
        pres = []
        for k in range(slots):
            cols = slice(k * BLOCK, (k + 1) * BLOCK)
            pres.append(
                sum(
                    p[pl.ds(pl.multiple_of((j ^ k_of) * rows, rows), rows), cols].astype(F32)
                    for k_of, p in zip(partners, part_refs)
                )
            )
        for u in range(union):
            value = jnp.zeros((rows, BLOCK), F32)
            bias = bias_ref[u : u + 1, :]
            for k in range(slots):
                value = jnp.where(mines[k] == float(u), jnp.maximum(pres[k] + bias, 0.0), value)
            spread[part, u * BLOCK : (u + 1) * BLOCK] = value.astype(BF16)
    step = 2 * BLOCK
    width = wout_ref.shape[1]
    hidden = spread[...]
    for n in range(0, width, step):
        product = jnp.dot(hidden, wout_ref[:, n : n + step], preferred_element_type=F32)
        terms[:, :, n : n + step] = product.reshape(count, rows, step)
    for turn in range(2):
        part = slice(turn * rows, (turn + 1) * rows)
        keep_ref[part, :] = terms[store ^ way_home(store, tensor, turn)]
        send_ref[part, :] = terms[store ^ way_home(store, tensor ^ 1, turn)]


WAY_HOME = (
    ((2, 1), (3, 0), (1, 2), (0, 3)),
    ((1, 3), (2, 0), (3, 1), (0, 2)),
    ((1, 0), (3, 2), (0, 1), (2, 3)),
    ((1, 3), (2, 0), (3, 1), (0, 2)),
)


def way_home(store, tensor, turn):
    code = sum(
        WAY_HOME[s][t][turn] << 2 * (4 * s + t) for s in range(4) for t in range(4)
    )
    code = jnp.int32(code - (1 << 32) if code >= 1 << 31 else code)
    return lax.shift_right_logical(code, 2 * (4 * store + tensor)) & 3


def fast(states, weight_in, bias_in, weight_out, bias_out, block_lists, union_blocks):
    count = lax.axis_size("store")
    width = weight_in.shape[0]
    rows = states.shape[0]
    slots = block_lists.shape[2]
    union = union_blocks.shape[1]
    total = union * BLOCK

    *chunks, union_ids = pl.pallas_call(
        functools.partial(split_kernel, count, width),
        out_shape=[VMEM((rows, width + BLOCK), BF16)] * count + [VMEM(union_blocks.shape, jnp.int32)],
        in_specs=[whole(pltpu.HBM)] * 3,
        out_specs=[whole(VMEM)] * (count + 1),
        scratch_shapes=[VMEM((slots, rows), jnp.int32), pltpu.SemaphoreType.DMA((count + 2,))],
        name="split_states",
    )(states, jnp.transpose(block_lists, (1, 2, 0))[0], union_blocks)

    def over_store(order, turn):
        return [
            (s * count + t, (s ^ order[t & 1][turn]) * count + t)
            for s in range(count) for t in range(count)
        ]

    got = [
        lax.ppermute(chunks[turn], ("store", "tensor"), over_store(ROUND_ONE, turn))
        for turn in range(count - 1)
    ] + [chunks[count - 1]]

    (win,) = gather(True, union_ids, weight_in, "gather_in")

    pre, ids = pl.pallas_call(
        functools.partial(first_kernel, count, slots),
        out_shape=[
            jax.ShapeDtypeStruct((count * rows, slots * BLOCK), BF16),
            jax.ShapeDtypeStruct((count * rows, BLOCK), F32),
        ],
        in_specs=[whole(VMEM)] * (count + 1),
        out_specs=[whole(VMEM)] * 2,
        scratch_shapes=[VMEM((count * rows, total), F32), VMEM((count * rows, width + BLOCK), BF16)],
        compiler_params=pltpu.CompilerParams(vmem_limit_bytes=40 * 2**20),
        name="first_dot",
    )(*got, win)

    parts = [
        lax.ppermute(pre, ("store", "tensor"), over_store(ROUND_TWO, turn))
        for turn in range(count - 1)
    ] + [pre]

    wout, bias = gather(False, union_ids, weight_out, "gather_out", bias_in.reshape(-1, BLOCK))

    keep, send = pl.pallas_call(
        functools.partial(second_kernel, count, slots),
        out_shape=[VMEM((count // 2 * rows, width), F32)] * 2,
        in_specs=[whole(VMEM)] * (count + 3),
        out_specs=[whole(VMEM)] * 2,
        scratch_shapes=[VMEM((count * rows, total), BF16), VMEM((count, rows, width), F32)],
        compiler_params=pltpu.CompilerParams(vmem_limit_bytes=40 * 2**20),
        name="second_dot",
    )(ids, bias, *parts, wout)

    pair = [(i, i ^ 1) for i in range(count)]
    both = (keep + lax.ppermute(send, "tensor", pair)).astype(BF16)

    def home(turn):
        return [
            (z * count + t, WAY_HOME[z][t][turn] * count + z)
            for z in range(count) for t in range(count)
        ]

    summed = sum(
        lax.ppermute(both[k * rows : (k + 1) * rows], ("store", "tensor"), home(k)).astype(F32)
        for k in range(count // 2)
    )
    return (summed + bias_out[None, :]).astype(BF16)


def general(states, weight_in, bias_in, weight_out, bias_out, block_lists, union_blocks):
    slice_width = weight_in.shape[0]
    union_ids = union_blocks[0]
    union_count = union_ids.shape[0]
    block_count = weight_in.shape[1] // BLOCK
    slot_count = block_lists.shape[2]
    own_rows = states.shape[0]
    sliced_states = lax.all_to_all(states, "store", split_axis=1, concat_axis=0, tiled=True)
    all_ids = lax.all_gather(block_lists, "store", axis=0, tiled=True)[:, 0, :]
    union_range = jnp.arange(union_count, dtype=jnp.int32)
    all_match = all_ids[:, :, None] == union_ids[None, None, :]
    all_keep = jnp.any(all_match, axis=-1)
    slot_pos = jnp.sum(jnp.where(all_match, union_range[None, None, :], 0), axis=-1)
    weight_in_union = jnp.take(
        weight_in.reshape(slice_width, block_count, BLOCK), union_ids, axis=1
    ).reshape(slice_width, union_count * BLOCK)
    weight_out_union = jnp.take(
        weight_out.reshape(block_count, BLOCK, slice_width), union_ids, axis=0
    ).reshape(union_count * BLOCK, slice_width)
    bias_blocks = bias_in.reshape(block_count, BLOCK)
    dense_pre = jnp.dot(sliced_states, weight_in_union, preferred_element_type=F32).reshape(
        own_rows * lax.axis_size("store"), union_count, BLOCK
    )
    picked = jnp.take_along_axis(dense_pre, slot_pos[:, :, None], axis=1)
    pre_act = lax.psum_scatter(
        (picked * all_keep[:, :, None].astype(F32)).reshape(
            own_rows * lax.axis_size("store"), slot_count * BLOCK
        ),
        "store",
        scatter_dimension=0,
        tiled=True,
    )
    own_ids = block_lists[:, 0, :]
    own_keep = jnp.any(own_ids[:, :, None] == union_ids[None, None, :], axis=-1)
    bias_rows = jnp.take(bias_blocks, jnp.maximum(own_ids, 0), axis=0).reshape(
        own_ids.shape[0], slot_count * BLOCK
    )
    active_mask = jnp.repeat(own_keep.astype(F32), BLOCK, axis=1)
    hidden = (jnp.maximum(pre_act + bias_rows, 0.0) * active_mask).astype(BF16)
    project_hidden = lax.all_gather(hidden, "store", axis=0, tiled=True)
    one_hot = jnp.logical_and(
        slot_pos[:, :, None] == union_range[None, None, :], all_keep[:, :, None]
    ).astype(BF16)
    spread = jnp.einsum(
        "rku,rkn->run",
        one_hot,
        project_hidden.reshape(-1, slot_count, BLOCK),
        preferred_element_type=F32,
    ).astype(BF16)
    partial_value = jnp.dot(
        spread.reshape(-1, union_count * BLOCK), weight_out_union, preferred_element_type=F32
    )
    row_terms = lax.all_to_all(partial_value, "store", split_axis=0, concat_axis=1, tiled=True)
    summed = lax.psum_scatter(row_terms, "tensor", scatter_dimension=1, tiled=True)
    return (summed + bias_out[None, :]).astype(BF16)


def solution(mesh):
    count = mesh.shape["store"]
    square = count == 4 and mesh.shape["tensor"] == 4
    return jax.shard_map(
        fast if square else general,
        mesh=mesh,
        in_specs=(
            P(("groups", "store"), None),
            P("store", "tensor"),
            P("tensor"),
            P("tensor", "store"),
            P("tensor"),
            P(("groups", "store"), "tensor", None),
            P(("groups", "tensor"), None),
        ),
        out_specs=P(("groups", "store"), "tensor"),
        check_vma=False,
    )
```

```python
import functools

import jax
import jax.numpy as jnp
from jax import lax
from jax.experimental import pallas as pl
from jax.experimental.pallas import tpu as pltpu
from jax.sharding import PartitionSpec as P

BLOCK = 128
BF16 = jnp.bfloat16
F32 = jnp.float32
VMEM = pltpu.VMEM


ROUND_ONE = ((2, 3, 1), (2, 3, 1))
ROUND_TWO = ((1, 2, 3), (3, 1, 2))


def partner(order, turn):
    odd = lax.axis_index("tensor") & 1
    return odd * order[1][turn] + (1 - odd) * order[0][turn]


def whole(space):
    return pl.BlockSpec(memory_space=space)


def split_kernel(count, width, states_ref, ids_ref, union_ref, *refs):
    out_refs, union_out, ids, sems = refs[:count], refs[count], refs[count + 1], refs[count + 2]
    me = lax.axis_index("store")
    ids_copy = pltpu.make_async_copy(ids_ref, ids, sems.at[count])
    ids_copy.start()
    copies = []
    for turn in range(count):
        other = me ^ partner(ROUND_ONE, turn) if turn < count - 1 else me
        start = pl.multiple_of(other * width, BLOCK)
        copies.append(
            pltpu.make_async_copy(
                states_ref.at[:, pl.ds(start, width)], out_refs[turn].at[:, :width], sems.at[turn]
            )
        )
        copies[-1].start()
    union_copy = pltpu.make_async_copy(union_ref, union_out, sems.at[count + 1])
    union_copy.start()
    slots, rows = ids_ref.shape
    ids_copy.wait()
    union_copy.wait()
    blocks, union = ids[...], union_out[...]
    places = jnp.full((slots, rows), -1.0, F32)
    for u in range(union.shape[1]):
        places = jnp.where(blocks == union[:, u : u + 1], float(u), places)
    padded = jnp.concatenate([places, jnp.full((BLOCK - slots, rows), -1.0, F32)], axis=0)
    tail = padded.T.astype(BF16)
    for k in range(count):
        out_refs[k][:, width:] = tail
    for copy in copies:
        copy.wait()


def gather_kernel(by_column, union_ref, weight_ref, *refs):
    *bias_refs, sems = refs
    out_ref = bias_refs.pop(len(bias_refs) // 2)
    union = union_ref.shape[1]
    copies = []
    for u in range(union):
        block = pl.ds(pl.multiple_of(union_ref[0, u] * BLOCK, BLOCK), BLOCK)
        place = pl.ds(u * BLOCK, BLOCK)
        if by_column:
            source, target = weight_ref.at[:, block], out_ref.at[:, place]
        else:
            source, target = weight_ref.at[block, :], out_ref.at[place, :]
        copies.append(pltpu.make_async_copy(source, target, sems.at[u]))
        copies[-1].start()
    if bias_refs:
        bias_ref, bias_out = bias_refs
        for u in range(union):
            bias_out[u : u + 1, :] = bias_ref[pl.ds(union_ref[0, u], 1), :]
    for copy in copies:
        copy.wait()


def gather(by_column, union_ids, weight, name, *bias):
    union = union_ids.shape[1]
    shape = (weight.shape[0], union * BLOCK) if by_column else (union * BLOCK, weight.shape[1])
    return pl.pallas_call(
        functools.partial(gather_kernel, by_column),
        out_shape=[VMEM(shape, BF16)] + [VMEM((union, BLOCK), F32)] * len(bias),
        in_specs=[whole(VMEM), whole(pltpu.HBM)] + [whole(VMEM)] * len(bias),
        out_specs=[whole(VMEM)] * (1 + len(bias)),
        scratch_shapes=[pltpu.SemaphoreType.DMA((union,))],
        compiler_params=pltpu.CompilerParams(vmem_limit_bytes=40 * 2**20),
        cost_estimate=pl.CostEstimate(flops=0, bytes_accessed=4 * shape[0] * shape[1], transcendentals=0),
        name=name,
    )(union_ids, weight, *bias)


def first_kernel(count, slots, *refs):
    chunk_refs = refs[:count]
    win_ref, pre_ref, ids_ref, dense, chunks = refs[count:]
    width, total = win_ref.shape
    rows = chunk_refs[0].shape[0]
    union = total // BLOCK
    for turn in range(count - 1):
        place = pl.multiple_of(partner(ROUND_ONE, turn) * rows, rows)
        chunks[pl.ds(place, rows), :] = chunk_refs[turn][...]
    chunks[:rows, :] = chunk_refs[count - 1][...]
    states = chunks[:, :width]
    ids = chunks[:, width:].astype(F32)
    ids_ref[...] = ids
    step = 2 * BLOCK
    for n in range(0, total, step):
        dense[:, n : n + step] = jnp.dot(states, win_ref[:, n : n + step], preferred_element_type=F32)
    for j in range(count):
        part = slice(j * rows, (j + 1) * rows)
        for k in range(slots):
            mine = jnp.broadcast_to(ids[part, k : k + 1], (rows, BLOCK))
            picked = jnp.zeros((rows, BLOCK), F32)
            for u in range(union):
                picked = jnp.where(mine == float(u), dense[part, u * BLOCK : (u + 1) * BLOCK], picked)
            pre_ref[part, k * BLOCK : (k + 1) * BLOCK] = picked.astype(pre_ref.dtype)


def second_kernel(count, slots, ids_ref, bias_ref, *refs):
    part_refs = refs[:count]
    partners = [partner(ROUND_TWO, turn) for turn in range(count - 1)] + [0]
    wout_ref = refs[count]
    keep_ref, send_ref, spread, terms = refs[count + 1 :]
    store, tensor = lax.axis_index("store"), lax.axis_index("tensor")
    rows = ids_ref.shape[0] // count
    union = bias_ref.shape[0]
    ids = ids_ref[...]
    for j in range(count):
        part = slice(j * rows, (j + 1) * rows)
        mines = [jnp.broadcast_to(ids[part, k : k + 1], (rows, BLOCK)) for k in range(slots)]
        pres = []
        for k in range(slots):
            cols = slice(k * BLOCK, (k + 1) * BLOCK)
            pres.append(
                sum(
                    p[pl.ds(pl.multiple_of((j ^ k_of) * rows, rows), rows), cols].astype(F32)
                    for k_of, p in zip(partners, part_refs)
                )
            )
        for u in range(union):
            value = jnp.zeros((rows, BLOCK), F32)
            bias = bias_ref[u : u + 1, :]
            for k in range(slots):
                value = jnp.where(mines[k] == float(u), jnp.maximum(pres[k] + bias, 0.0), value)
            spread[part, u * BLOCK : (u + 1) * BLOCK] = value.astype(BF16)
    step = 2 * BLOCK
    width = wout_ref.shape[1]
    hidden = spread[...]
    for n in range(0, width, step):
        product = jnp.dot(hidden, wout_ref[:, n : n + step], preferred_element_type=F32)
        terms[:, :, n : n + step] = product.reshape(count, rows, step)
    for turn in range(2):
        part = slice(turn * rows, (turn + 1) * rows)
        keep_ref[part, :] = terms[store ^ way_home(store, tensor, turn)]
        send_ref[part, :] = terms[store ^ way_home(store, tensor ^ 1, turn)]


WAY_HOME = (
    ((2, 1), (3, 0), (1, 2), (0, 3)),
    ((1, 3), (2, 0), (3, 1), (0, 2)),
    ((1, 0), (3, 2), (0, 1), (2, 3)),
    ((1, 3), (0, 2), (3, 1), (2, 0)),
)


def way_home(store, tensor, turn):
    code = sum(
        WAY_HOME[s][t][turn] << 2 * (4 * s + t) for s in range(4) for t in range(4)
    )
    code = jnp.int32(code - (1 << 32) if code >= 1 << 31 else code)
    return lax.shift_right_logical(code, 2 * (4 * store + tensor)) & 3


def fast(states, weight_in, bias_in, weight_out, bias_out, block_lists, union_blocks):
    count = lax.axis_size("store")
    width = weight_in.shape[0]
    rows = states.shape[0]
    slots = block_lists.shape[2]
    union = union_blocks.shape[1]
    total = union * BLOCK

    *chunks, union_ids = pl.pallas_call(
        functools.partial(split_kernel, count, width),
        out_shape=[VMEM((rows, width + BLOCK), BF16)] * count + [VMEM(union_blocks.shape, jnp.int32)],
        in_specs=[whole(pltpu.HBM)] * 3,
        out_specs=[whole(VMEM)] * (count + 1),
        scratch_shapes=[VMEM((slots, rows), jnp.int32), pltpu.SemaphoreType.DMA((count + 2,))],
        name="split_states",
    )(states, jnp.transpose(block_lists, (1, 2, 0))[0], union_blocks)

    def over_store(order, turn):
        return [
            (s * count + t, (s ^ order[t & 1][turn]) * count + t)
            for s in range(count) for t in range(count)
        ]

    got = [
        lax.ppermute(chunks[turn], ("store", "tensor"), over_store(ROUND_ONE, turn))
        for turn in range(count - 1)
    ] + [chunks[count - 1]]

    (win,) = gather(True, union_ids, weight_in, "gather_in")

    pre, ids = pl.pallas_call(
        functools.partial(first_kernel, count, slots),
        out_shape=[
            jax.ShapeDtypeStruct((count * rows, slots * BLOCK), BF16),
            jax.ShapeDtypeStruct((count * rows, BLOCK), F32),
        ],
        in_specs=[whole(VMEM)] * (count + 1),
        out_specs=[whole(VMEM)] * 2,
        scratch_shapes=[VMEM((count * rows, total), F32), VMEM((count * rows, width + BLOCK), BF16)],
        compiler_params=pltpu.CompilerParams(vmem_limit_bytes=40 * 2**20),
        name="first_dot",
    )(*got, win)

    parts = [
        lax.ppermute(pre, ("store", "tensor"), over_store(ROUND_TWO, turn))
        for turn in range(count - 1)
    ] + [pre]

    wout, bias = gather(False, union_ids, weight_out, "gather_out", bias_in.reshape(-1, BLOCK))

    keep, send = pl.pallas_call(
        functools.partial(second_kernel, count, slots),
        out_shape=[VMEM((count // 2 * rows, width), F32)] * 2,
        in_specs=[whole(VMEM)] * (count + 3),
        out_specs=[whole(VMEM)] * 2,
        scratch_shapes=[VMEM((count * rows, total), BF16), VMEM((count, rows, width), F32)],
        compiler_params=pltpu.CompilerParams(vmem_limit_bytes=40 * 2**20),
        name="second_dot",
    )(ids, bias, *parts, wout)

    pair = [(i, i ^ 1) for i in range(count)]
    both = (keep + lax.ppermute(send, "tensor", pair)).astype(BF16)

    def home(turn):
        return [
            (z * count + t, WAY_HOME[z][t][turn] * count + z)
            for z in range(count) for t in range(count)
        ]

    summed = sum(
        lax.ppermute(both[k * rows : (k + 1) * rows], ("store", "tensor"), home(k)).astype(F32)
        for k in range(count // 2)
    )
    return (summed + bias_out[None, :]).astype(BF16)


def general(states, weight_in, bias_in, weight_out, bias_out, block_lists, union_blocks):
    slice_width = weight_in.shape[0]
    union_ids = union_blocks[0]
    union_count = union_ids.shape[0]
    block_count = weight_in.shape[1] // BLOCK
    slot_count = block_lists.shape[2]
    own_rows = states.shape[0]
    sliced_states = lax.all_to_all(states, "store", split_axis=1, concat_axis=0, tiled=True)
    all_ids = lax.all_gather(block_lists, "store", axis=0, tiled=True)[:, 0, :]
    union_range = jnp.arange(union_count, dtype=jnp.int32)
    all_match = all_ids[:, :, None] == union_ids[None, None, :]
    all_keep = jnp.any(all_match, axis=-1)
    slot_pos = jnp.sum(jnp.where(all_match, union_range[None, None, :], 0), axis=-1)
    weight_in_union = jnp.take(
        weight_in.reshape(slice_width, block_count, BLOCK), union_ids, axis=1
    ).reshape(slice_width, union_count * BLOCK)
    weight_out_union = jnp.take(
        weight_out.reshape(block_count, BLOCK, slice_width), union_ids, axis=0
    ).reshape(union_count * BLOCK, slice_width)
    bias_blocks = bias_in.reshape(block_count, BLOCK)
    dense_pre = jnp.dot(sliced_states, weight_in_union, preferred_element_type=F32).reshape(
        own_rows * lax.axis_size("store"), union_count, BLOCK
    )
    picked = jnp.take_along_axis(dense_pre, slot_pos[:, :, None], axis=1)
    pre_act = lax.psum_scatter(
        (picked * all_keep[:, :, None].astype(F32)).reshape(
            own_rows * lax.axis_size("store"), slot_count * BLOCK
        ),
        "store",
        scatter_dimension=0,
        tiled=True,
    )
    own_ids = block_lists[:, 0, :]
    own_keep = jnp.any(own_ids[:, :, None] == union_ids[None, None, :], axis=-1)
    bias_rows = jnp.take(bias_blocks, jnp.maximum(own_ids, 0), axis=0).reshape(
        own_ids.shape[0], slot_count * BLOCK
    )
    active_mask = jnp.repeat(own_keep.astype(F32), BLOCK, axis=1)
    hidden = (jnp.maximum(pre_act + bias_rows, 0.0) * active_mask).astype(BF16)
    project_hidden = lax.all_gather(hidden, "store", axis=0, tiled=True)
    one_hot = jnp.logical_and(
        slot_pos[:, :, None] == union_range[None, None, :], all_keep[:, :, None]
    ).astype(BF16)
    spread = jnp.einsum(
        "rku,rkn->run",
        one_hot,
        project_hidden.reshape(-1, slot_count, BLOCK),
        preferred_element_type=F32,
    ).astype(BF16)
    partial_value = jnp.dot(
        spread.reshape(-1, union_count * BLOCK), weight_out_union, preferred_element_type=F32
    )
    row_terms = lax.all_to_all(partial_value, "store", split_axis=0, concat_axis=1, tiled=True)
    summed = lax.psum_scatter(row_terms, "tensor", scatter_dimension=1, tiled=True)
    return (summed + bias_out[None, :]).astype(BF16)


def solution(mesh):
    count = mesh.shape["store"]
    square = count == 4 and mesh.shape["tensor"] == 4
    return jax.shard_map(
        fast if square else general,
        mesh=mesh,
        in_specs=(
            P(("groups", "store"), None),
            P("store", "tensor"),
            P("tensor"),
            P("tensor", "store"),
            P("tensor"),
            P(("groups", "store"), "tensor", None),
            P(("groups", "tensor"), None),
        ),
        out_specs=P(("groups", "store"), "tensor"),
        check_vma=False,
    )
```
